32 devices in a mesh: ctx: 16 (over z, y, core), head: 2 (over x).
Axes of the slice: x: 2, y: 2, z: 4, core: 2. Of those that a mesh axis runs over, the one named last changes fastest.
Arguments:
- queries_nope: bfloat16 [1024, 8192], P('ctx', 'head'), may hold values from -4 to 4
- queries_rope: bfloat16 [1024, 4096], P('ctx', 'head'), may hold values from -128 to 128
- latents: bfloat16 [1024, 512], P('ctx'), may hold values from -8 to 8
- rope_keys: bfloat16 [1024, 64], P('ctx'), may hold values from -4 to 4
- positions: int32 [1024], P('ctx'), may hold values from 0 to 1535
- key_up: bfloat16 [512, 8192], P(None, 'head'), may hold values from -0.5 to 0.5
- value_up: bfloat16 [512, 8192], P(None, 'head'), may hold values from -0.25 to 0.25
- out_proj: bfloat16 [8192, 3584], P('head', 'ctx'), may hold values from -0.0625 to 0.0625
Outputs:
- attended: bfloat16 [1024, 3584], P('ctx', 'head')
The draws below stay inside these ranges and needn't reach their ends.
All inputs are finite; a program needn't handle non-finite values.
Results may differ from the reference program's by a relative error of at most 0.014.
The reference program's roundings to bfloat16 on the way count: a program that leaves them out, or rounds other values in their place, can miss the bound.
Values may be sent and summed in bfloat16 or wider, within the bound.
A program may use at most 128 MiB of HBM per device.

```python
import math
import jax
import jax.numpy as jnp
from jax import lax

LATENT = 512
ROPE = 64
NOPE = 128
VDIM = 128
H = 64
DOUT = 3584
TOKENS = 1024


def draw_queries_nope(key, part):
    draw_key = jax.random.fold_in(key, 21)
    values = jnp.clip(jax.random.normal(draw_key, (TOKENS, H * NOPE)), -4.0, 4.0)
    return values.astype(jnp.bfloat16)


def draw_queries_rope(key, part):
    draw_key = jax.random.fold_in(key, 22)
    values = jnp.clip(jax.random.normal(draw_key, (TOKENS, H * ROPE)), -4.0, 4.0)
    return values.astype(jnp.bfloat16)


def draw_rope_keys(key, part):
    draw_key = jax.random.fold_in(key, 23)
    values = jnp.clip(jax.random.normal(draw_key, (TOKENS, ROPE)), -4.0, 4.0)
    return values.astype(jnp.bfloat16)


def draw_positions(key, part):
    order = jax.random.permutation(jax.random.fold_in(key, 24), TOKENS - 1)
    gaps = jnp.where(order < TOKENS // 2, 2, 1).astype(jnp.int32)
    start = jnp.zeros((1,), jnp.int32)
    return jnp.concatenate([start, jnp.cumsum(gaps).astype(jnp.int32)]).astype(jnp.int32)


def levels(key, extent, cuts, least, top_value):
    def one(position, blocks):
        draws = jax.random.uniform(jax.random.fold_in(jax.random.fold_in(key, 6), position), (blocks,), jnp.float32, least / len(cuts), top_value / len(cuts))
        return jnp.repeat(jnp.exp(draws), extent[position] // blocks).reshape((-1,) + (1,) * (len(extent) - position - 1))

    factor_of = one(*cuts[0])
    for cut in cuts[1:]:
        factor_of = factor_of * one(*cut)
    return factor_of


def noise(own_key, extent, scale, most, cuts=(), held_as=jnp.bfloat16):
    result = jax.random.normal(own_key, extent, jnp.float32) * scale
    if len(cuts) > 0:
        result = levels(own_key, extent, cuts, -0.22, 0.18) * result
    return jnp.clip(result, min=-most, max=most).astype(held_as)


def setup_inputs(seed: int = 0) -> dict:
    splits = jax.random.split(jax.random.key(seed), 9)
    return {
        "queries_nope": draw_queries_nope(jax.random.fold_in(splits[8], 71), 0),
        "queries_rope": draw_queries_rope(jax.random.fold_in(splits[8], 71), 0),
        "latents": noise(splits[2], (TOKENS, LATENT), 1.5, 8.0, ((0, 16),)),
        "rope_keys": draw_rope_keys(jax.random.fold_in(splits[8], 71), 0),
        "positions": draw_positions(jax.random.fold_in(splits[8], 71), 0),
        "key_up": noise(splits[5], (LATENT, H * NOPE), NOPE ** -0.5, 0.5, ((1, 2),)),
        "value_up": noise(splits[6], (LATENT, H * VDIM), LATENT ** -0.5, 0.25, ((1, 2),)),
        "out_proj": noise(splits[7], (H * VDIM, DOUT), (H * VDIM) ** -0.5, 0.0625, ((0, 2), (1, 16))),
    }


masked_value = -1e+30

def rope_tables(token_pos, width):
    half_width = width // 2
    freqs = jnp.exp(jnp.arange(half_width, dtype=jnp.float32) * (-2.0 * math.log(10000.0) / width))
    angle = token_pos.astype(jnp.float32)[:, None] * freqs[None, :]
    return (jnp.cos(angle), jnp.sin(angle))

def rotate(values, cosine, sine):
    half_width = values.shape[-1] // 2
    first_half = values[..., :half_width]
    second_half = values[..., half_width:]
    cos_part = cosine[:, None, :]
    sin_part = sine[:, None, :]
    return jnp.concatenate([first_half * cos_part - second_half * sin_part, second_half * cos_part + first_half * sin_part], axis=-1)

def reference(queries_nope, queries_rope, latents, rope_keys, positions, key_up, value_up, out_proj):
    scale = 1.0 / math.sqrt(NOPE + ROPE)
    cosine, sine = rope_tables(positions, ROPE)
    rot_queries = rotate(queries_rope.astype(jnp.float32).reshape(TOKENS, H, ROPE), cosine, sine).astype(jnp.bfloat16)
    rot_keys = rotate(rope_keys.astype(jnp.float32)[:, None, :], cosine, sine)[:, 0, :].astype(jnp.bfloat16)
    lat_queries = jnp.einsum('thn,lhn->thl', queries_nope.astype(jnp.float32).reshape(TOKENS, H, NOPE), key_up.astype(jnp.float32).reshape(LATENT, H, NOPE)).astype(jnp.bfloat16)
    visible = positions[None, :] <= positions[:, None]

    def one_head(index):
        lat_part = lat_queries[:, index, :]
        rope_part = rot_queries[:, index, :]
        scores = jnp.dot(lat_part, latents.T, preferred_element_type=jnp.float32) + jnp.dot(rope_part, rot_keys.T, preferred_element_type=jnp.float32)
        scores = jnp.where(visible, scores * scale, masked_value)
        peak = lax.optimization_barrier(jnp.max(scores, axis=1))
        weights = jnp.where(visible, jnp.exp(scores - peak[:, None]), 0.0)
        totals = lax.optimization_barrier(jnp.sum(weights, axis=1))
        summed = jnp.dot(weights.astype(jnp.bfloat16), latents, preferred_element_type=jnp.float32)
        return (summed / totals[:, None]).astype(jnp.bfloat16)
    latent_out = lax.map(one_head, jnp.arange(H))
    head_out = jnp.einsum('htl,lhd->thd', latent_out.astype(jnp.float32), value_up.astype(jnp.float32).reshape(LATENT, H, VDIM)).astype(jnp.bfloat16)
    head_out = head_out.reshape(TOKENS, H * VDIM)
    return jnp.dot(head_out, out_proj, preferred_element_type=jnp.float32).astype(jnp.bfloat16)
```

```python
import math

import jax
import jax.numpy as jnp
from jax import lax
from jax.sharding import PartitionSpec as P

LATENT = 512
ROPE = 64
NOPE = 128
VDIM = 128


masked_value = -1e30


def rope_tables(token_pos, width):
    half_width = width // 2
    freqs = jnp.exp(jnp.arange(half_width, dtype=jnp.float32) * (-2.0 * math.log(10000.0) / width))
    angle = token_pos.astype(jnp.float32)[:, None] * freqs[None, :]
    return (jnp.cos(angle), jnp.sin(angle))


def rotate(values, cosine, sine):
    half_width = values.shape[-1] // 2
    first_half = values[..., :half_width]
    second_half = values[..., half_width:]
    cos_part = cosine[:, None, :]
    sin_part = sine[:, None, :]
    return jnp.concatenate(
        [
            first_half * cos_part - second_half * sin_part,
            second_half * cos_part + first_half * sin_part,
        ],
        axis=-1,
    )


def attend(lat_rows, rope_rows, query_index, latents, rot_keys):
    scale = 1.0 / math.sqrt(NOPE + ROPE)
    both = lax.all_gather(jnp.concatenate([latents, rot_keys], axis=1), "ctx", axis=0, tiled=True)
    keys = both[:, :LATENT]
    scores = jnp.einsum(
        "rl,kl->rk",
        jnp.concatenate([lat_rows, rope_rows], axis=1),
        both,
        preferred_element_type=jnp.float32,
    )
    visible = jnp.arange(both.shape[0])[None, :] <= query_index[:, None]
    scores = jnp.where(visible, scores * scale, masked_value)
    peak = jnp.max(scores, axis=1)
    weights = jnp.where(visible, jnp.exp(scores - peak[:, None]), 0.0)
    totals = jnp.sum(weights, axis=1)
    summed = jnp.dot(weights.astype(jnp.bfloat16), keys, preferred_element_type=jnp.float32)
    return (summed / totals[:, None]).astype(jnp.bfloat16)


def upward(latent_out, value_up, token_count, head_count):
    head_out = jnp.einsum(
        "thl,lhd->thd",
        latent_out.reshape(token_count, head_count, LATENT),
        value_up.reshape(LATENT, head_count, VDIM),
        preferred_element_type=jnp.float32,
    )
    return head_out.astype(jnp.bfloat16).reshape(token_count, head_count * VDIM)


def body(queries_nope, queries_rope, latents, rope_keys, positions, key_up, value_up, out_proj):
    token_count = latents.shape[0]
    head_count = key_up.shape[1] // NOPE
    cosine, sine = rope_tables(positions, ROPE)
    rot_queries = rotate(
        queries_rope.astype(jnp.float32).reshape(token_count, head_count, ROPE), cosine, sine
    ).astype(jnp.bfloat16)
    rot_keys = rotate(rope_keys.astype(jnp.float32)[:, None, :], cosine, sine)[:, 0, :].astype(
        jnp.bfloat16
    )
    lat_queries = jnp.einsum(
        "thn,lhn->thl",
        queries_nope.reshape(token_count, head_count, NOPE),
        key_up.reshape(LATENT, head_count, NOPE),
        preferred_element_type=jnp.float32,
    ).astype(jnp.bfloat16)
    lat_rows = lat_queries.reshape(token_count * head_count, LATENT)
    rope_rows = rot_queries.reshape(token_count * head_count, ROPE)
    first = lax.axis_index("ctx") * token_count
    query_index = jnp.repeat(first + jnp.arange(token_count), head_count)
    latent_out = attend(lat_rows, rope_rows, query_index, latents, rot_keys)
    head_out = upward(latent_out, value_up, token_count, head_count)
    partial_sums = jnp.dot(
        lax.all_gather(head_out, "ctx", axis=0, tiled=True),
        out_proj,
        preferred_element_type=jnp.float32,
    ).astype(jnp.bfloat16)
    columns = lax.all_to_all(partial_sums, "ctx", split_axis=0, concat_axis=1, tiled=True)
    return lax.psum_scatter(columns, "head", scatter_dimension=1, tiled=True)


def solution(mesh):
    in_specs = (
        P("ctx", "head"),
        P("ctx", "head"),
        P("ctx", None),
        P("ctx", None),
        P("ctx"),
        P(None, "head"),
        P(None, "head"),
        P("head", "ctx"),
    )
    out_specs = P("ctx", "head")
    return jax.shard_map(body, mesh=mesh, in_specs=in_specs, out_specs=out_specs, check_vma=False)
```

```python
import functools
import math

import jax
import jax.numpy as jnp
from jax import lax
from jax.experimental import pallas as pl
from jax.experimental.pallas import tpu as pltpu
from jax.sharding import PartitionSpec as P

LATENT = 512
ROPE = 64
NOPE = 128
VDIM = 128
KEYW = 640
CORES = 2
LINES = 2
GROUP = 4

masked_value = -1e30
MESH = pl.DeviceIdType.MESH
NT = (((1,), (1,)), ((), ()))


def rope_tables(token_pos, width):
    half_width = width // 2
    freqs = jnp.exp(jnp.arange(half_width, dtype=jnp.float32) * (-2.0 * math.log(10000.0) / width))
    angle = token_pos.astype(jnp.float32)[:, None] * freqs[None, :]
    return (jnp.cos(angle), jnp.sin(angle))


def rotate(values, cosine, sine):
    half_width = values.shape[-1] // 2
    first_half = values[..., :half_width]
    second_half = values[..., half_width:]
    cos_part = cosine[:, None, :]
    sin_part = sine[:, None, :]
    return jnp.concatenate(
        [
            first_half * cos_part - second_half * sin_part,
            second_half * cos_part + first_half * sin_part,
        ],
        axis=-1,
    )


def kernel(
    n_ctx,
    n_head,
    kv_in,
    qn_ref,
    qr_ref,
    key_up_hbm,
    value_up_hbm,
    proj_hbm,
    out_ref,
    key_up,
    value_up,
    proj,
    kv,
    query,
    ho,
    acc,
    out_send,
    land,
    load_sem,
    proj_send,
    proj_recv,
    kv_send_z,
    kv_send_y,
    kv_send_c,
    kv_recv,
    ho_send_z,
    ho_send_y,
    ho_recv,
    back_send,
    land_recv,
):
    tokens = kv_in.shape[0]
    n_z = n_ctx // (CORES * LINES)
    groups = ho.shape[1]
    pairs = land.shape[1]
    me = lax.axis_index("ctx")
    head = lax.axis_index("head")
    core = lax.rem(me, CORES)
    line = lax.rem(me // CORES, LINES)
    z = me // (CORES * LINES)
    other_line = 1 - line
    owner_head = me // (2 * pairs)
    slot = lax.rem(me // CORES, pairs)

    def ctx_of(z_at, line_at, core_at):
        return (z_at * LINES + line_at) * CORES + core_at

    core_peer = (ctx_of(z, line, 1 - core), head)
    line_peer = (ctx_of(z, other_line, core), head)

    def z_peer(step):
        return lax.rem(z + step, n_z)

    barrier = pltpu.get_barrier_semaphore()
    n_class = (n_ctx // CORES) * n_head
    mine = (me // CORES) * n_head + head

    def greet(step, carry):
        other = lax.rem(mine + step, n_class)
        there = ((other // n_head) * CORES + core, lax.rem(other, n_head))
        pl.semaphore_signal(barrier, inc=1, device_id=there, device_id_type=MESH)
        return carry

    lax.fori_loop(1, n_class, greet, 0)
    pl.semaphore_signal(barrier, inc=1, device_id=core_peer, device_id_type=MESH)

    load_key = pltpu.make_async_copy(key_up_hbm, key_up, load_sem.at[0])
    load_value = pltpu.make_async_copy(value_up_hbm, value_up, load_sem.at[1])
    load_proj = pltpu.make_async_copy(proj_hbm, proj.at[core], load_sem.at[2])
    load_key.start()
    load_value.start()
    load_proj.start()
    pl.semaphore_wait(barrier, n_class)

    def kv_copy(src, origin, send_sem, there):
        return pltpu.make_async_remote_copy(
            src_ref=src,
            dst_ref=kv.at[origin],
            send_sem=send_sem,
            recv_sem=kv_recv.at[origin],
            device_id=there,
            device_id_type=MESH,
        )

    sends = []
    for step in range(1, n_z):
        there = (ctx_of(z_peer(step), line, core), head)
        sends.append(kv_copy(kv_in, me, kv_send_z.at[step - 1], there))
        sends[-1].start()
    sends.append(kv_copy(kv_in, me, kv_send_y.at[0], line_peer))
    sends[-1].start()
    sends.append(kv_copy(kv_in, me, kv_send_c.at[0, 0], core_peer))
    sends[-1].start()
    kv[me] = kv_in[...]

    proj_copy = pltpu.make_async_remote_copy(
        src_ref=proj_hbm,
        dst_ref=proj.at[core],
        send_sem=proj_send,
        recv_sem=proj_recv.at[core],
        device_id=core_peer,
        device_id_type=MESH,
    )

    load_key.wait()

    def up(group, carry):
        for part in range(GROUP):
            columns = pl.ds(pl.multiple_of((group * GROUP + part) * NOPE, NOPE), NOPE)
            rows = pl.ds(part * tokens, tokens)
            query[group, rows, pl.ds(0, LATENT)] = lax.dot_general(
                qn_ref[:, columns], key_up[:, columns], NT, preferred_element_type=jnp.float32
            ).astype(jnp.bfloat16)
        query[group, :, pl.ds(LATENT, KEYW - LATENT)] = qr_ref[group]
        return carry

    lax.fori_loop(0, groups, up, 0)

    def kv_wait(origin):
        kv_copy(kv_in, origin, kv_send_y.at[0], line_peer).wait_recv()

    for step in range(1, n_z):
        origin = ctx_of(z_peer(step), line, core)
        kv_wait(origin)
        sends.append(kv_copy(kv.at[origin], origin, kv_send_y.at[step], line_peer))
        sends[-1].start()
        sends.append(kv_copy(kv.at[origin], origin, kv_send_c.at[0, step], core_peer))
        sends[-1].start()
    for step in range(n_z):
        origin = ctx_of(z_peer(step), other_line, core)
        kv_wait(origin)
        sends.append(kv_copy(kv.at[origin], origin, kv_send_c.at[1, step], core_peer))
        sends[-1].start()
    proj_copy.start()
    for step in range(n_z):
        for line_at in (line, other_line):
            kv_wait(ctx_of(z_peer(step), line_at, 1 - core))
    load_value.wait()

    def ho_copy(line_at, group, z_at, send_sem, there):
        return pltpu.make_async_remote_copy(
            src_ref=ho.at[line_at, group, z_at],
            dst_ref=ho.at[line_at, group, z_at],
            send_sem=send_sem,
            recv_sem=ho_recv.at[line_at, group, z_at],
            device_id=there,
            device_id_type=MESH,
        )

    scale = 1.0 / math.sqrt(NOPE + ROPE)
    n_keys = n_ctx * tokens
    n_rows = GROUP * tokens

    def attend(group, carry):
        keys = kv[...].reshape(n_keys, KEYW)
        scores = lax.dot_general(query[group], keys, NT, preferred_element_type=jnp.float32)
        row = lax.broadcasted_iota(jnp.int32, (n_rows, 1), 0)
        last = me * tokens + lax.rem(row, tokens)
        key_index = lax.broadcasted_iota(jnp.int32, (n_rows, n_keys), 1)
        scores = jnp.where(key_index <= last, scores * scale, masked_value)
        peak = jnp.max(scores, axis=1, keepdims=True)
        weights = jnp.exp(scores - peak)
        totals = jnp.sum(weights, axis=1, keepdims=True)
        summed = jnp.dot(
            weights.astype(jnp.bfloat16), keys[:, :LATENT], preferred_element_type=jnp.float32
        )
        latent_out = (summed / totals).astype(jnp.bfloat16)
        for part in range(GROUP):
            columns = pl.ds(pl.multiple_of((group * GROUP + part) * VDIM, VDIM), VDIM)
            ho[line, group, z, :, pl.ds(part * VDIM, VDIM)] = jnp.dot(
                latent_out[part * tokens : (part + 1) * tokens],
                value_up[:, columns],
                preferred_element_type=jnp.float32,
            ).astype(jnp.bfloat16)
        for step in range(1, n_z):
            there = (ctx_of(z_peer(step), line, core), head)
            ho_copy(line, group, z, ho_send_z.at[group, step - 1], there).start()
        ho_copy(line, group, z, ho_send_y.at[group, 0], line_peer).start()
        return carry

    lax.fori_loop(0, groups, attend, 0)

    def forward(group, carry):
        for step in range(1, n_z):
            z_at = z_peer(step)
            copy = ho_copy(line, group, z_at, ho_send_y.at[group, step], line_peer)
            copy.wait_recv()
            copy.start()
        return carry

    lax.fori_loop(0, groups, forward, 0)

    load_proj.wait()
    pltpu.make_async_remote_copy(
        src_ref=proj_hbm,
        dst_ref=proj.at[1 - core],
        send_sem=proj_send,
        recv_sem=proj_recv.at[1 - core],
        device_id=core_peer,
        device_id_type=MESH,
    ).wait_recv()

    def project(line_at, waits):
        acc[...] = jnp.zeros_like(acc)

        def add(group, carry):
            if waits:
                for step in range(n_z):
                    z_at = z_peer(step)
                    ho_copy(line_at, group, z_at, ho_send_y.at[group, step], line_peer).wait_recv()
            block = ho[line_at, group].reshape(n_z * tokens, GROUP * VDIM)
            depth = pl.ds(pl.multiple_of(group * (GROUP * VDIM), GROUP * VDIM), GROUP * VDIM)
            for half in range(CORES):
                acc[half] += jnp.dot(block, proj[half, depth, :], preferred_element_type=jnp.float32)
            return carry

        lax.fori_loop(0, groups, add, 0)
        for z_at in range(n_z):
            for half in range(CORES):
                out_send[line_at, z_at, half] = acc[half, pl.ds(z_at * tokens, tokens), :].astype(
                    jnp.bfloat16
                )

    def back(line_at, z_at):
        return pltpu.make_async_remote_copy(
            src_ref=out_send.at[line_at, z_at],
            dst_ref=land.at[head, slot],
            send_sem=back_send.at[line_at, z_at],
            recv_sem=land_recv.at[head, slot],
            device_id=(ctx_of(z_at, line_at, core), owner_head),
            device_id_type=MESH,
        )

    stays = owner_head == head

    project(line, False)
    for step in range(1, n_z):
        back(line, z_peer(step)).start()

    @pl.when(stays)
    def _():
        pltpu.make_async_copy(
            out_send.at[line, z], land.at[head, slot], land_recv.at[head, slot]
        ).start()

    @pl.when(jnp.logical_not(stays))
    def _():
        back(line, z).start()

    project(other_line, True)
    for step in range(n_z):
        back(other_line, z_peer(step)).start()

    for part in range(n_head):
        for pair in range(pairs):
            pltpu.make_async_copy(
                out_send.at[0, 0], land.at[part, pair], land_recv.at[part, pair]
            ).wait()
    for pair in range(pairs):
        total = land[0, pair].astype(jnp.float32)
        for part in range(1, n_head):
            total = total + land[part, pair].astype(jnp.float32)
        out_ref[pair] = total.astype(out_ref.dtype)

    for copy in sends:
        copy.wait_send()
    proj_copy.wait_send()

    def drain(group, carry):
        for step in range(1, n_z):
            ho_copy(line, group, z, ho_send_z.at[group, step - 1], line_peer).wait_send()
        for step in range(n_z):
            ho_copy(line, group, z_peer(step), ho_send_y.at[group, step], line_peer).wait_send()
        return carry

    lax.fori_loop(0, groups, drain, 0)
    for step in range(1, n_z):
        back(line, z_peer(step)).wait_send()

    @pl.when(jnp.logical_not(stays))
    def _():
        back(line, z).wait_send()

    for step in range(n_z):
        back(other_line, z_peer(step)).wait_send()


def body(
    n_ctx,
    n_head,
    queries_nope,
    queries_rope,
    latents,
    rope_keys,
    positions,
    key_up,
    value_up,
    out_proj,
):
    tokens = latents.shape[0]
    heads = key_up.shape[1] // NOPE
    groups = heads // GROUP
    n_z = n_ctx // (CORES * LINES)
    pairs = n_ctx // (CORES * n_head)
    width = out_proj.shape[1]
    bf16 = jnp.bfloat16
    cosine, sine = rope_tables(positions, ROPE)
    rot_queries = rotate(
        queries_rope.astype(jnp.float32).reshape(tokens, heads, ROPE), cosine, sine
    ).astype(bf16)
    rot_queries = jnp.pad(
        rot_queries.transpose(1, 0, 2).reshape(groups, GROUP * tokens, ROPE),
        ((0, 0), (0, 0), (0, KEYW - LATENT - ROPE)),
    )
    rot_keys = rotate(rope_keys.astype(jnp.float32)[:, None, :], cosine, sine)[:, 0, :].astype(bf16)
    kv_in = jnp.pad(
        jnp.concatenate([latents, rot_keys], axis=1), ((0, 0), (0, KEYW - LATENT - ROPE))
    )
    vmem = pl.BlockSpec(memory_space=pltpu.VMEM)
    hbm = pl.BlockSpec(memory_space=pl.ANY)
    dma = pltpu.SemaphoreType.DMA
    rows = n_ctx * tokens * heads * tokens
    out = pl.pallas_call(
        functools.partial(kernel, n_ctx, n_head),
        out_shape=jax.ShapeDtypeStruct((pairs, CORES, tokens, width), bf16),
        in_specs=[vmem, vmem, vmem, hbm, hbm, hbm],
        out_specs=vmem,
        scratch_shapes=[
            pltpu.VMEM(key_up.shape, bf16),
            pltpu.VMEM(value_up.shape, bf16),
            pltpu.VMEM((CORES,) + out_proj.shape, bf16),
            pltpu.VMEM((n_ctx, tokens, KEYW), bf16),
            pltpu.VMEM((groups, GROUP * tokens, KEYW), bf16),
            pltpu.VMEM((LINES, groups, n_z, tokens, GROUP * VDIM), bf16),
            pltpu.VMEM((CORES, n_z * tokens, width), jnp.float32),
            pltpu.VMEM((LINES, n_z, CORES, tokens, width), bf16),
            pltpu.VMEM((n_head, pairs, CORES, tokens, width), bf16),
            dma((3,)),
            dma,
            dma((CORES,)),
            dma((n_z,)),
            dma((n_z,)),
            dma((LINES, n_z)),
            dma((n_ctx,)),
            dma((groups, n_z)),
            dma((groups, n_z)),
            dma((LINES, groups, n_z)),
            dma((LINES, n_z)),
            dma((n_head, pairs)),
        ],
        compiler_params=pltpu.CompilerParams(
            collective_id=0, has_side_effects=True, vmem_limit_bytes=52 * 1024 * 1024
        ),
        cost_estimate=pl.CostEstimate(
            flops=2 * rows * (KEYW + LATENT), bytes_accessed=1 << 24, transcendentals=rows
        ),
    )(kv_in, queries_nope, rot_queries, key_up, value_up, out_proj)
    return out.transpose(2, 0, 1, 3).reshape(tokens, pairs * CORES * width)


def solution(mesh):
    in_specs = (
        P("ctx", "head"),
        P("ctx", "head"),
        P("ctx", None),
        P("ctx", None),
        P("ctx"),
        P(None, "head"),
        P(None, "head"),
        P("head", "ctx"),
    )
    out_specs = P("ctx", "head")
    run = functools.partial(body, mesh.shape["ctx"], mesh.shape["head"])
    return jax.shard_map(run, mesh=mesh, in_specs=in_specs, out_specs=out_specs, check_vma=False)
```

```python
import functools
import math

import jax
import jax.numpy as jnp
from jax import lax
from jax.experimental import pallas as pl
from jax.experimental.pallas import tpu as pltpu
from jax.sharding import PartitionSpec as P

LATENT = 512
ROPE = 64
NOPE = 128
VDIM = 128
KEYW = 640
CORES = 2
LINES = 2
GROUP = 4
LAG = 1

masked_value = -1e30
MESH = pl.DeviceIdType.MESH
NT = (((1,), (1,)), ((), ()))


def rope_tables(token_pos, width):
    half_width = width // 2
    freqs = jnp.exp(jnp.arange(half_width, dtype=jnp.float32) * (-2.0 * math.log(10000.0) / width))
    angle = token_pos.astype(jnp.float32)[:, None] * freqs[None, :]
    return (jnp.cos(angle), jnp.sin(angle))


def swap_halves(values):
    lane = lax.broadcasted_iota(jnp.int32, values.shape, 1)
    ahead = pltpu.roll(values, 2 * ROPE - ROPE // 2, 1)
    behind = pltpu.roll(values, ROPE // 2, 1)
    return jnp.where(lax.rem(lane, ROPE) < ROPE // 2, ahead, behind)


def kernel(
    n_ctx,
    n_head,
    lat_ref,
    rk_ref,
    cos_ref,
    sin_ref,
    qn_ref,
    qr_ref,
    key_up_hbm,
    value_up_hbm,
    proj_hbm,
    out_ref,
    key_up,
    value_up,
    proj,
    kv,
    query,
    ho,
    acc,
    out_send,
    land,
    load_sem,
    proj_send,
    proj_recv,
    kv_send_z,
    kv_send_y,
    kv_send_c,
    kv_recv,
    ho_send_z,
    ho_send_y,
    ho_recv,
    back_send,
    land_recv,
):
    tokens = lat_ref.shape[0]
    n_z = n_ctx // (CORES * LINES)
    groups = ho.shape[1]
    pairs = land.shape[1]
    me = lax.axis_index("ctx")
    head = lax.axis_index("head")
    core = lax.rem(me, CORES)
    line = lax.rem(me // CORES, LINES)
    z = me // (CORES * LINES)
    other_line = 1 - line
    owner_head = me // (2 * pairs)
    slot = lax.rem(me // CORES, pairs)

    def ctx_of(z_at, line_at, core_at):
        return (z_at * LINES + line_at) * CORES + core_at

    core_peer = (ctx_of(z, line, 1 - core), head)
    line_peer = (ctx_of(z, other_line, core), head)

    def z_peer(step):
        return lax.rem(z + step, n_z)

    barrier = pltpu.get_barrier_semaphore()
    n_class = (n_ctx // CORES) * n_head
    mine = (me // CORES) * n_head + head

    def greet(step, carry):
        other = lax.rem(mine + step, n_class)
        there = ((other // n_head) * CORES + core, lax.rem(other, n_head))
        pl.semaphore_signal(barrier, inc=1, device_id=there, device_id_type=MESH)
        return carry

    lax.fori_loop(1, n_class, greet, 0)
    pl.semaphore_signal(barrier, inc=1, device_id=core_peer, device_id_type=MESH)

    load_key = pltpu.make_async_copy(key_up_hbm, key_up, load_sem.at[0])
    load_value = pltpu.make_async_copy(value_up_hbm, value_up, load_sem.at[1])
    load_proj = pltpu.make_async_copy(proj_hbm, proj.at[core], load_sem.at[2])
    load_key.start()
    load_value.start()
    load_proj.start()
    pl.semaphore_wait(barrier, n_class)

    def kv_copy(src, origin, send_sem, there):
        return pltpu.make_async_remote_copy(
            src_ref=src,
            dst_ref=kv.at[origin],
            send_sem=send_sem,
            recv_sem=kv_recv.at[origin],
            device_id=there,
            device_id_type=MESH,
        )

    def rotated(values):
        values = values.astype(jnp.float32)
        return values * cos_ref[...] + swap_halves(values) * sin_ref[...]

    kv[me, :, pl.ds(0, LATENT)] = lat_ref[...]
    kv[me, :, pl.ds(LATENT, KEYW - LATENT)] = rotated(rk_ref[...]).astype(jnp.bfloat16)

    sends = []

    def send_if(allowed, origin, send_sem, there):
        copy = kv_copy(kv.at[origin], origin, send_sem, there)
        sends.append((allowed, copy))
        if allowed is None:
            copy.start()
        else:
            pl.when(allowed)(copy.start)

    for step in range(1, n_z):
        there = (ctx_of(lax.rem(z + step, n_z), line, core), head)
        send_if(z + step < n_z, me, kv_send_z.at[step - 1], there)
    send_if(None, me, kv_send_y.at[0], line_peer)
    send_if(None, me, kv_send_c.at[0, 0], core_peer)
    for step in range(1, n_z):

        @pl.when(z + step < n_z)
        def _():
            later = pl.ds((z + step) * (LINES * CORES), LINES * CORES)
            kv[later] = jnp.zeros((LINES * CORES, tokens, KEYW), jnp.bfloat16)

    proj_copy = pltpu.make_async_remote_copy(
        src_ref=proj_hbm,
        dst_ref=proj.at[core],
        send_sem=proj_send,
        recv_sem=proj_recv.at[core],
        device_id=core_peer,
        device_id_type=MESH,
    )

    load_key.wait()

    def up(group, carry):
        for part in range(GROUP):
            columns = pl.ds(pl.multiple_of((group * GROUP + part) * NOPE, NOPE), NOPE)
            rows = pl.ds(part * tokens, tokens)
            query[group, rows, pl.ds(0, LATENT)] = lax.dot_general(
                qn_ref[:, columns], key_up[:, columns], NT, preferred_element_type=jnp.float32
            ).astype(jnp.bfloat16)
        for pair in range(GROUP // 2):
            start = pl.multiple_of((group * (GROUP // 2) + pair) * 2 * ROPE, 2 * ROPE)
            both = rotated(qr_ref[:, pl.ds(start, 2 * ROPE)])
            for part, turned in ((0, both), (1, pltpu.roll(both, ROPE, 1))):
                rows = pl.ds((2 * pair + part) * tokens, tokens)
                query[group, rows, pl.ds(LATENT, KEYW - LATENT)] = turned.astype(jnp.bfloat16)
        return carry

    lax.fori_loop(0, groups, up, 0)

    def kv_wait(origin):
        kv_copy(kv.at[origin], origin, kv_send_y.at[0], line_peer).wait_recv()

    def earlier(step):
        return lax.rem(z + n_z - step, n_z)

    for step in range(1, n_z):
        origin = ctx_of(earlier(step), line, core)
        allowed = z >= step
        pl.when(allowed)(functools.partial(kv_wait, origin))
        send_if(allowed, origin, kv_send_y.at[step], line_peer)
        send_if(allowed, origin, kv_send_c.at[0, step], core_peer)
    for step in range(n_z):
        origin = ctx_of(earlier(step), other_line, core)
        allowed = z >= step
        pl.when(allowed)(functools.partial(kv_wait, origin))
        send_if(allowed, origin, kv_send_c.at[1, step], core_peer)
    proj_copy.start()
    for step in range(n_z):
        for line_at in (line, other_line):
            origin = ctx_of(earlier(step), line_at, 1 - core)
            pl.when(z >= step)(functools.partial(kv_wait, origin))
    load_value.wait()

    def ho_copy(line_at, group, z_at, send_sem, there):
        return pltpu.make_async_remote_copy(
            src_ref=ho.at[line_at, group, z_at],
            dst_ref=ho.at[line_at, group, z_at],
            send_sem=send_sem,
            recv_sem=ho_recv.at[line_at, group, z_at],
            device_id=there,
            device_id_type=MESH,
        )

    scale = math.log2(math.e) / math.sqrt(NOPE + ROPE)
    n_rows = GROUP * tokens

    def attend(group, blocks):
        n_keys = blocks * tokens
        keys = kv[pl.ds(0, blocks)].reshape(n_keys, KEYW)
        scores = lax.dot_general(query[group], keys, NT, preferred_element_type=jnp.float32)
        row = lax.broadcasted_iota(jnp.int32, (n_rows, 1), 0)
        last = me * tokens + lax.rem(row, tokens)
        key_index = lax.broadcasted_iota(jnp.int32, (n_rows, n_keys), 1)
        scores = jnp.where(key_index <= last, scores, masked_value)
        peak = jnp.max(scores, axis=1, keepdims=True)
        weights = jnp.exp2((scores - peak) * scale)
        totals = jnp.sum(weights, axis=1, keepdims=True)
        summed = jnp.dot(
            weights.astype(jnp.bfloat16), keys[:, :LATENT], preferred_element_type=jnp.float32
        )
        latent_out = (summed * (1.0 / totals)).astype(jnp.bfloat16)
        for part in range(GROUP):
            columns = pl.ds(pl.multiple_of((group * GROUP + part) * VDIM, VDIM), VDIM)
            ho[line, group, z, :, pl.ds(part * VDIM, VDIM)] = jnp.dot(
                latent_out[part * tokens : (part + 1) * tokens],
                value_up[:, columns],
                preferred_element_type=jnp.float32,
            ).astype(jnp.bfloat16)

    above = z + 1 < n_z
    below = z >= 1
    up_peer = (ctx_of(lax.rem(z + 1, n_z), line, core), head)
    down_peer = (ctx_of(lax.rem(z + n_z - 1, n_z), line, core), head)

    def up_copy(group, z_at):
        return ho_copy(line, group, z_at, ho_send_z.at[0, group, z_at], up_peer)

    def down_copy(group, z_at):
        return ho_copy(line, group, z_at, ho_send_z.at[1, group, z_at], down_peer)

    def line_copy(group, z_at):
        return ho_copy(line, group, z_at, ho_send_y.at[group, z_at], line_peer)

    def tick(time, carry):
        @pl.when(time < groups)
        def _():
            pl.when(2 * z < n_z)(functools.partial(attend, time, n_ctx // 2))
            pl.when(2 * z >= n_z)(functools.partial(attend, time, n_ctx))
            pl.when(above)(lambda: up_copy(time, z).start())
            pl.when(below)(lambda: down_copy(time, z).start())
            line_copy(time, z).start()

        for step in range(1, n_z):
            group = time - step - LAG
            in_time = jnp.logical_and(group >= 0, group < groups)

            @pl.when(jnp.logical_and(in_time, z >= step))
            def _():
                line_copy(group, z - step).wait_recv()
                pl.when(above)(lambda: up_copy(group, z - step).start())
                line_copy(group, z - step).start()

            @pl.when(jnp.logical_and(in_time, z + step < n_z))
            def _():
                line_copy(group, z + step).wait_recv()
                pl.when(below)(lambda: down_copy(group, z + step).start())
                line_copy(group, z + step).start()

        return carry

    lax.fori_loop(0, groups + n_z - 1 + LAG, tick, 0)

    load_proj.wait()
    pltpu.make_async_remote_copy(
        src_ref=proj_hbm,
        dst_ref=proj.at[1 - core],
        send_sem=proj_send,
        recv_sem=proj_recv.at[1 - core],
        device_id=core_peer,
        device_id_type=MESH,
    ).wait_recv()

    def project(line_at, waits):
        acc[...] = jnp.zeros_like(acc)

        def add(group, carry):
            if waits:
                for step in range(n_z):
                    z_at = z_peer(step)
                    ho_copy(line_at, group, z_at, ho_send_y.at[group, step], line_peer).wait_recv()
            block = ho[line_at, group].reshape(n_z * tokens, GROUP * VDIM)
            depth = pl.ds(pl.multiple_of(group * (GROUP * VDIM), GROUP * VDIM), GROUP * VDIM)
            for half in range(CORES):
                acc[half] += lax.dot_general(
                    block, proj[half, :, depth], NT, preferred_element_type=jnp.float32
                )
            return carry

        lax.fori_loop(0, groups, add, 0)
        for z_at in range(n_z):
            for half in range(CORES):
                out_send[line_at, z_at, half] = acc[half, pl.ds(z_at * tokens, tokens), :].astype(
                    jnp.bfloat16
                )

    def back(line_at, z_at):
        return pltpu.make_async_remote_copy(
            src_ref=out_send.at[line_at, z_at],
            dst_ref=land.at[head, slot],
            send_sem=back_send.at[line_at, z_at],
            recv_sem=land_recv.at[head, slot],
            device_id=(ctx_of(z_at, line_at, core), owner_head),
            device_id_type=MESH,
        )

    stays = owner_head == head

    project(line, False)
    for step in range(1, n_z):
        back(line, z_peer(step)).start()

    @pl.when(stays)
    def _():
        pltpu.make_async_copy(
            out_send.at[line, z], land.at[head, slot], land_recv.at[head, slot]
        ).start()

    @pl.when(jnp.logical_not(stays))
    def _():
        back(line, z).start()

    project(other_line, True)
    for step in range(n_z):
        back(other_line, z_peer(step)).start()

    for part in range(n_head):
        for pair in range(pairs):
            pltpu.make_async_copy(
                out_send.at[0, 0], land.at[part, pair], land_recv.at[part, pair]
            ).wait()
    for pair in range(pairs):
        total = land[0, pair].astype(jnp.float32)
        for part in range(1, n_head):
            total = total + land[part, pair].astype(jnp.float32)
        out_ref[pair] = total.astype(out_ref.dtype)

    for allowed, copy in sends:
        if allowed is None:
            copy.wait_send()
        else:
            pl.when(allowed)(copy.wait_send)
    proj_copy.wait_send()

    def drain(group, carry):
        for z_at in range(n_z):
            line_copy(group, z_at).wait_send()
            pl.when(jnp.logical_and(above, z >= z_at))(up_copy(group, z_at).wait_send)
            pl.when(jnp.logical_and(below, z <= z_at))(down_copy(group, z_at).wait_send)
        return carry

    lax.fori_loop(0, groups, drain, 0)
    for step in range(1, n_z):
        back(line, z_peer(step)).wait_send()

    @pl.when(jnp.logical_not(stays))
    def _():
        back(line, z).wait_send()

    for step in range(n_z):
        back(other_line, z_peer(step)).wait_send()


def body(
    n_ctx,
    n_head,
    queries_nope,
    queries_rope,
    latents,
    rope_keys,
    positions,
    key_up,
    value_up,
    out_proj,
):
    tokens = latents.shape[0]
    heads = key_up.shape[1] // NOPE
    groups = heads // GROUP
    n_z = n_ctx // (CORES * LINES)
    pairs = n_ctx // (CORES * n_head)
    width = out_proj.shape[1]
    bf16 = jnp.bfloat16
    cosine, sine = rope_tables(positions, ROPE)
    cosine = jnp.concatenate([cosine] * 4, axis=1)
    sine = jnp.concatenate([-sine, sine] * 2, axis=1)
    rope_keys = jnp.pad(rope_keys, ((0, 0), (0, KEYW - LATENT - ROPE)))
    out_proj = out_proj.T
    vmem = pl.BlockSpec(memory_space=pltpu.VMEM)
    hbm = pl.BlockSpec(memory_space=pl.ANY)
    dma = pltpu.SemaphoreType.DMA
    rows = n_ctx * tokens * heads * tokens
    out = pl.pallas_call(
        functools.partial(kernel, n_ctx, n_head),
        out_shape=jax.ShapeDtypeStruct((pairs, CORES, tokens, width), bf16),
        in_specs=[vmem] * 6 + [hbm] * 3,
        out_specs=vmem,
        scratch_shapes=[
            pltpu.VMEM(key_up.shape, bf16),
            pltpu.VMEM(value_up.shape, bf16),
            pltpu.VMEM((CORES,) + out_proj.shape, bf16),
            pltpu.VMEM((n_ctx, tokens, KEYW), bf16),
            pltpu.VMEM((groups, GROUP * tokens, KEYW), bf16),
            pltpu.VMEM((LINES, groups, n_z, tokens, GROUP * VDIM), bf16),
            pltpu.VMEM((CORES, n_z * tokens, width), jnp.float32),
            pltpu.VMEM((LINES, n_z, CORES, tokens, width), bf16),
            pltpu.VMEM((n_head, pairs, CORES, tokens, width), bf16),
            dma((3,)),
            dma,
            dma((CORES,)),
            dma((n_z,)),
            dma((n_z,)),
            dma((LINES, n_z)),
            dma((n_ctx,)),
            dma((2, groups, n_z)),
            dma((groups, n_z)),
            dma((LINES, groups, n_z)),
            dma((LINES, n_z)),
            dma((n_head, pairs)),
        ],
        compiler_params=pltpu.CompilerParams(
            collective_id=0, has_side_effects=True, vmem_limit_bytes=52 * 1024 * 1024
        ),
        cost_estimate=pl.CostEstimate(
            flops=2 * rows * (KEYW + LATENT), bytes_accessed=1 << 24, transcendentals=rows
        ),
    )(latents, rope_keys, cosine, sine, queries_nope, queries_rope, key_up, value_up, out_proj)
    return out.transpose(2, 0, 1, 3).reshape(tokens, pairs * CORES * width)


def solution(mesh):
    in_specs = (
        P("ctx", "head"),
        P("ctx", "head"),
        P("ctx", None),
        P("ctx", None),
        P("ctx"),
        P(None, "head"),
        P(None, "head"),
        P("head", "ctx"),
    )
    out_specs = P("ctx", "head")
    run = functools.partial(body, mesh.shape["ctx"], mesh.shape["head"])
    return jax.shard_map(run, mesh=mesh, in_specs=in_specs, out_specs=out_specs, check_vma=False)
```

```python
import functools
import math

import jax
import jax.numpy as jnp
from jax import lax
from jax.experimental import pallas as pl
from jax.experimental.pallas import tpu as pltpu
from jax.sharding import PartitionSpec as P

LATENT = 512
ROPE = 64
NOPE = 128
VDIM = 128
KEYW = 640
CORES = 2
LINES = 2
GROUP = 8
SPLIT = 2
CHUNKS = 4
LAG = 1

masked_value = -1e30
MESH = pl.DeviceIdType.MESH
NT = (((1,), (1,)), ((), ()))


def rope_tables(token_pos, width):
    half_width = width // 2
    freqs = jnp.exp(jnp.arange(half_width, dtype=jnp.float32) * (-2.0 * math.log(10000.0) / width))
    angle = token_pos.astype(jnp.float32)[:, None] * freqs[None, :]
    return (jnp.cos(angle), jnp.sin(angle))


def swap_halves(values):
    lane = lax.broadcasted_iota(jnp.int32, values.shape, 1)
    ahead = pltpu.roll(values, 2 * ROPE - ROPE // 2, 1)
    behind = pltpu.roll(values, ROPE // 2, 1)
    return jnp.where(lax.rem(lane, ROPE) < ROPE // 2, ahead, behind)


def kernel(
    n_ctx,
    n_head,
    lat_hbm,
    rk_hbm,
    cos_ref,
    sin_ref,
    qn_hbm,
    qr_hbm,
    key_up_hbm,
    value_up_hbm,
    proj_hbm,
    out_ref,
    lat_ref,
    rk_ref,
    wide,
    qn_ref,
    qr_ref,
    key_up,
    value_up,
    proj,
    kv,
    query,
    ho,
    acc,
    out_send,
    land,
    load_sem,
    proj_send_c,
    proj_send_y,
    proj_send_d,
    proj_recv_c,
    proj_recv_y,
    proj_recv_d,
    kv_send_z,
    kv_send_y,
    kv_send_c,
    kv_recv,
    ho_send_z,
    ho_recv,
    back_send,
    land_recv,
):
    tokens = lat_ref.shape[0]
    n_z = n_ctx // (CORES * LINES)
    sub = tokens // SPLIT
    ticks = ho.shape[0]
    groups = ticks // SPLIT
    depth = proj_hbm.shape[1]
    spots = land.shape[1]
    me = lax.axis_index("ctx")
    head = lax.axis_index("head")
    core = lax.rem(me, CORES)
    line = lax.rem(me // CORES, LINES)
    z = me // (CORES * LINES)
    other_line = 1 - line
    owner_head = z // spots
    slot = lax.rem(z, spots)

    def ctx_of(z_at, line_at, core_at):
        return (z_at * LINES + line_at) * CORES + core_at

    core_peer = (ctx_of(z, line, 1 - core), head)
    line_peer = (ctx_of(z, other_line, core), head)

    def z_peer(step):
        return lax.rem(z + step, n_z)

    barrier = pltpu.get_barrier_semaphore()
    n_class = (n_ctx // CORES) * n_head
    mine = (me // CORES) * n_head + head

    def greet(step, carry):
        other = lax.rem(mine + step, n_class)
        there = ((other // n_head) * CORES + core, lax.rem(other, n_head))
        pl.semaphore_signal(barrier, inc=1, device_id=there, device_id_type=MESH)
        return carry

    lax.fori_loop(1, n_class, greet, 0)
    pl.semaphore_signal(barrier, inc=1, device_id=core_peer, device_id_type=MESH)

    loads = []
    for source, target in (
        (lat_hbm, lat_ref),
        (rk_hbm, rk_ref),
        (qn_hbm, qn_ref),
        (qr_hbm, qr_ref),
        (key_up_hbm, key_up),
        (value_up_hbm, value_up),
        (proj_hbm, proj.at[line, core]),
    ):
        loads.append(pltpu.make_async_copy(source, target, load_sem.at[len(loads)]))
        loads[-1].start()
    load_lat, load_rk, load_qn, load_qr, load_key, load_value, load_proj = loads
    wide[...] = jnp.zeros_like(wide)
    load_lat.wait()
    load_rk.wait()
    wide[:, pl.ds(0, ROPE)] = rk_ref[...].astype(jnp.float32)
    pl.semaphore_wait(barrier, n_class)

    def kv_copy(src, origin, send_sem, there):
        return pltpu.make_async_remote_copy(
            src_ref=src,
            dst_ref=kv.at[origin],
            send_sem=send_sem,
            recv_sem=kv_recv.at[origin],
            device_id=there,
            device_id_type=MESH,
        )

    def rotated(values):
        values = values.astype(jnp.float32)
        return values * cos_ref[...] + swap_halves(values) * sin_ref[...]

    kv[me, :, pl.ds(0, LATENT)] = lat_ref[...]
    kv[me, :, pl.ds(LATENT, KEYW - LATENT)] = rotated(wide[...]).astype(jnp.bfloat16)

    sends = []

    def send_if(allowed, origin, send_sem, there):
        copy = kv_copy(kv.at[origin], origin, send_sem, there)
        sends.append((allowed, copy))
        if allowed is None:
            copy.start()
        else:
            pl.when(allowed)(copy.start)

    for step in range(1, n_z):
        there = (ctx_of(lax.rem(z + step, n_z), line, core), head)
        send_if(z + step < n_z, me, kv_send_z.at[step - 1], there)
    send_if(None, me, kv_send_y.at[0], line_peer)
    send_if(None, me, kv_send_c.at[0, 0], core_peer)
    for step in range(1, n_z):

        @pl.when(z + step < n_z)
        def _():
            later = pl.ds((z + step) * (LINES * CORES), LINES * CORES)
            kv[later] = jnp.zeros((LINES * CORES, tokens, KEYW), jnp.bfloat16)

    def chunk_of(index):
        return pl.ds(index * (depth // CHUNKS), depth // CHUNKS)

    proj_core = pltpu.make_async_remote_copy(
        src_ref=proj_hbm,
        dst_ref=proj.at[line, core],
        send_sem=proj_send_c,
        recv_sem=proj_recv_c,
        device_id=core_peer,
        device_id_type=MESH,
    )

    def proj_line(index):
        return pltpu.make_async_remote_copy(
            src_ref=proj_hbm.at[:, chunk_of(index)],
            dst_ref=proj.at[line, core, :, chunk_of(index)],
            send_sem=proj_send_y.at[index],
            recv_sem=proj_recv_y.at[index],
            device_id=line_peer,
            device_id_type=MESH,
        )

    def proj_across(index):
        return pltpu.make_async_remote_copy(
            src_ref=proj.at[other_line, core, :, chunk_of(index)],
            dst_ref=proj.at[other_line, core, :, chunk_of(index)],
            send_sem=proj_send_d.at[index],
            recv_sem=proj_recv_d.at[index],
            device_id=core_peer,
            device_id_type=MESH,
        )

    load_qn.wait()
    load_qr.wait()
    load_key.wait()

    def up(group, carry):
        for part in range(GROUP):
            columns = pl.ds(pl.multiple_of((group * GROUP + part) * NOPE, NOPE), NOPE)
            made = lax.dot_general(
                qn_ref[:, columns], key_up[:, columns], NT, preferred_element_type=jnp.float32
            ).astype(jnp.bfloat16)
            for half in range(SPLIT):
                query[half * groups + group, pl.ds(part * sub, sub), pl.ds(0, LATENT)] = made[
                    half * sub : (half + 1) * sub
                ]
        for pair in range(GROUP // 2):
            start = pl.multiple_of((group * (GROUP // 2) + pair) * 2 * ROPE, 2 * ROPE)
            both = rotated(qr_ref[:, pl.ds(start, 2 * ROPE)])
            for part, turned in ((0, both), (1, pltpu.roll(both, ROPE, 1))):
                rows = pl.ds((2 * pair + part) * sub, sub)
                turned = turned.astype(jnp.bfloat16)
                for half in range(SPLIT):
                    query[half * groups + group, rows, pl.ds(LATENT, KEYW - LATENT)] = turned[
                        half * sub : (half + 1) * sub
                    ]
        return carry

    lax.fori_loop(0, groups, up, 0)

    def kv_wait(origin):
        kv_copy(kv.at[origin], origin, kv_send_y.at[0], line_peer).wait_recv()

    def earlier(step):
        return lax.rem(z + n_z - step, n_z)

    for step in range(1, n_z):
        origin = ctx_of(earlier(step), line, core)
        allowed = z >= step
        pl.when(allowed)(functools.partial(kv_wait, origin))
        send_if(allowed, origin, kv_send_y.at[step], line_peer)
        send_if(allowed, origin, kv_send_c.at[0, step], core_peer)
    for index in range(CHUNKS):
        proj_line(index).start()
    for step in range(n_z):
        origin = ctx_of(earlier(step), other_line, core)
        allowed = z >= step
        pl.when(allowed)(functools.partial(kv_wait, origin))
        send_if(allowed, origin, kv_send_c.at[1, step], core_peer)
    proj_core.start()
    for step in range(n_z):
        for line_at in (line, other_line):
            origin = ctx_of(earlier(step), line_at, 1 - core)
            pl.when(z >= step)(functools.partial(kv_wait, origin))
    load_value.wait()

    above = z + 1 < n_z
    below = z >= 1
    up_peer = (ctx_of(lax.rem(z + 1, n_z), line, core), head)
    down_peer = (ctx_of(lax.rem(z + n_z - 1, n_z), line, core), head)

    def ho_copy(way, time, z_at, there):
        return pltpu.make_async_remote_copy(
            src_ref=ho.at[time, z_at],
            dst_ref=ho.at[time, z_at],
            send_sem=ho_send_z.at[way, time, z_at],
            recv_sem=ho_recv.at[time, z_at],
            device_id=there,
            device_id_type=MESH,
        )

    def up_copy(time, z_at):
        return ho_copy(0, time, z_at, up_peer)

    def down_copy(time, z_at):
        return ho_copy(1, time, z_at, down_peer)

    scale = math.log2(math.e) / math.sqrt(NOPE + ROPE)
    n_rows = GROUP * sub

    def attend(time, blocks):
        half = time // groups
        group = lax.rem(time, groups)
        n_keys = blocks * tokens
        keys = kv[pl.ds(0, blocks)].reshape(n_keys, KEYW)
        scores = lax.dot_general(query[time], keys, NT, preferred_element_type=jnp.float32)
        row = lax.broadcasted_iota(jnp.int32, (n_rows, 1), 0)
        last = me * tokens + half * sub + lax.rem(row, sub)
        key_index = lax.broadcasted_iota(jnp.int32, (n_rows, n_keys), 1)
        scores = jnp.where(key_index <= last, scores, masked_value)
        peak = jnp.max(scores, axis=1, keepdims=True)
        weights = jnp.exp2((scores - peak) * scale)
        totals = jnp.sum(weights, axis=1, keepdims=True)
        summed = jnp.dot(
            weights.astype(jnp.bfloat16), keys[:, :LATENT], preferred_element_type=jnp.float32
        )
        latent_out = (summed * (1.0 / totals)).astype(jnp.bfloat16)
        for part in range(GROUP):
            columns = pl.ds(pl.multiple_of((group * GROUP + part) * VDIM, VDIM), VDIM)
            ho[time, z, :, pl.ds(part * VDIM, VDIM)] = jnp.dot(
                latent_out[part * sub : (part + 1) * sub],
                value_up[:, columns],
                preferred_element_type=jnp.float32,
            ).astype(jnp.bfloat16)

    def tick(time, carry):
        @pl.when(time < ticks)
        def _():
            pl.when(2 * z < n_z)(functools.partial(attend, time, n_ctx // 2))
            pl.when(2 * z >= n_z)(functools.partial(attend, time, n_ctx))
            pl.when(above)(lambda: up_copy(time, z).start())
            pl.when(below)(lambda: down_copy(time, z).start())

        for step in range(1, n_z - 1):
            past = time - step - LAG
            in_time = jnp.logical_and(past >= 0, past < ticks)

            @pl.when(jnp.logical_and(in_time, jnp.logical_and(z >= step, above)))
            def _():
                up_copy(past, z - step).wait_recv()
                up_copy(past, z - step).start()

            @pl.when(jnp.logical_and(in_time, jnp.logical_and(z + step < n_z, below)))
            def _():
                down_copy(past, z + step).wait_recv()
                down_copy(past, z + step).start()

        for index in range(CHUNKS):

            @pl.when(time == 3 + 2 * index)
            def _():
                proj_line(index).wait_recv()
                proj_across(index).start()

        return carry

    lax.fori_loop(0, max(ticks + n_z - 2 + LAG, 2 * CHUNKS + 2), tick, 0)

    load_proj.wait()
    proj_core.wait_recv()
    for index in range(CHUNKS):
        proj_across(index).wait_recv()

    def back(half, z_at):
        return pltpu.make_async_remote_copy(
            src_ref=out_send.at[half, z_at],
            dst_ref=land.at[head, slot, half],
            send_sem=back_send.at[half, z_at],
            recv_sem=land_recv.at[head, slot, half],
            device_id=(ctx_of(z_at, line, core), owner_head),
            device_id_type=MESH,
        )

    stays = owner_head == head

    for half in range(SPLIT):
        acc[...] = jnp.zeros_like(acc)

        def add(group, carry):
            time = half * groups + group
            for step in range(1, n_z):

                @pl.when(jnp.logical_and(z >= step, jnp.logical_or(z == n_z - 1, step == n_z - 1)))
                def _():
                    up_copy(time, z - step).wait_recv()

                @pl.when(jnp.logical_and(z + step < n_z, jnp.logical_or(z == 0, step == n_z - 1)))
                def _():
                    down_copy(time, z + step).wait_recv()

            block = ho[time].reshape(n_z * sub, GROUP * VDIM)
            span = pl.ds(pl.multiple_of(group * (GROUP * VDIM), GROUP * VDIM), GROUP * VDIM)
            for line_at in range(LINES):
                for core_at in range(CORES):
                    acc[line_at, core_at] += lax.dot_general(
                        block,
                        proj[line_at, core_at, :, span],
                        NT,
                        preferred_element_type=jnp.float32,
                    )
            return carry

        lax.fori_loop(0, groups, add, 0)
        for z_at in range(n_z):
            out_send[half, z_at] = acc[:, :, pl.ds(z_at * sub, sub), :].astype(jnp.bfloat16)
        for step in range(1, n_z):
            back(half, z_peer(step)).start()

        @pl.when(stays)
        def _():
            pltpu.make_async_copy(
                out_send.at[half, z], land.at[head, slot, half], land_recv.at[head, slot, half]
            ).start()

        @pl.when(jnp.logical_not(stays))
        def _():
            back(half, z).start()

    for half in range(SPLIT):
        for part in range(n_head):
            for spot in range(spots):
                pltpu.make_async_copy(
                    out_send.at[0, 0], land.at[part, spot, half], land_recv.at[part, spot, half]
                ).wait()
        columns = []
        for spot in range(spots):
            for line_at in range(LINES):
                for core_at in range(CORES):
                    total = land[0, spot, half, line_at, core_at].astype(jnp.float32)
                    for part in range(1, n_head):
                        total += land[part, spot, half, line_at, core_at].astype(jnp.float32)
                    columns.append(total)
        out_ref[pl.ds(half * sub, sub), :] = jnp.concatenate(columns, axis=1).astype(out_ref.dtype)

    for allowed, copy in sends:
        if allowed is None:
            copy.wait_send()
        else:
            pl.when(allowed)(copy.wait_send)
    proj_core.wait_send()
    for index in range(CHUNKS):
        proj_line(index).wait_send()
        proj_across(index).wait_send()

    def drain(time, carry):
        for z_at in range(n_z):
            pl.when(jnp.logical_and(above, z >= z_at))(up_copy(time, z_at).wait_send)
            pl.when(jnp.logical_and(below, z <= z_at))(down_copy(time, z_at).wait_send)
        return carry

    lax.fori_loop(0, ticks, drain, 0)
    for half in range(SPLIT):
        for step in range(1, n_z):
            back(half, z_peer(step)).wait_send()
        pl.when(jnp.logical_not(stays))(back(half, z).wait_send)


def body(
    n_ctx,
    n_head,
    queries_nope,
    queries_rope,
    latents,
    rope_keys,
    positions,
    key_up,
    value_up,
    out_proj,
):
    tokens = latents.shape[0]
    heads = key_up.shape[1] // NOPE
    groups = heads // GROUP
    n_z = n_ctx // (CORES * LINES)
    spots = n_z // n_head
    sub = tokens // SPLIT
    width = out_proj.shape[1]
    bf16 = jnp.bfloat16
    cosine, sine = rope_tables(positions, ROPE)
    cosine = jnp.concatenate([cosine] * 4, axis=1)
    sine = jnp.concatenate([-sine, sine] * 2, axis=1)
    out_proj = out_proj.T
    vmem = pl.BlockSpec(memory_space=pltpu.VMEM)
    hbm = pl.BlockSpec(memory_space=pl.ANY)
    dma = pltpu.SemaphoreType.DMA
    rows = n_ctx * tokens * heads * tokens
    return pl.pallas_call(
        functools.partial(kernel, n_ctx, n_head),
        out_shape=jax.ShapeDtypeStruct((tokens, spots * LINES * CORES * width), bf16),
        in_specs=[hbm] * 2 + [vmem] * 2 + [hbm] * 5,
        out_specs=vmem,
        scratch_shapes=[
            pltpu.VMEM(latents.shape, bf16),
            pltpu.VMEM(rope_keys.shape, bf16),
            pltpu.VMEM((tokens, KEYW - LATENT), jnp.float32),
            pltpu.VMEM(queries_nope.shape, bf16),
            pltpu.VMEM(queries_rope.shape, bf16),
            pltpu.VMEM(key_up.shape, bf16),
            pltpu.VMEM(value_up.shape, bf16),
            pltpu.VMEM((LINES, CORES) + out_proj.shape, bf16),
            pltpu.VMEM((n_ctx, tokens, KEYW), bf16),
            pltpu.VMEM((SPLIT * groups, GROUP * sub, KEYW), bf16),
            pltpu.VMEM((SPLIT * groups, n_z, sub, GROUP * VDIM), bf16),
            pltpu.VMEM((LINES, CORES, n_z * sub, width), jnp.float32),
            pltpu.VMEM((SPLIT, n_z, LINES, CORES, sub, width), bf16),
            pltpu.VMEM((n_head, spots, SPLIT, LINES, CORES, sub, width), bf16),
            dma((7,)),
            dma,
            dma((CHUNKS,)),
            dma((CHUNKS,)),
            dma,
            dma((CHUNKS,)),
            dma((CHUNKS,)),
            dma((n_z,)),
            dma((n_z,)),
            dma((LINES, n_z)),
            dma((n_ctx,)),
            dma((2, SPLIT * groups, n_z)),
            dma((SPLIT * groups, n_z)),
            dma((SPLIT, n_z)),
            dma((n_head, spots, SPLIT)),
        ],
        compiler_params=pltpu.CompilerParams(
            collective_id=0, has_side_effects=True, vmem_limit_bytes=52 * 1024 * 1024
        ),
        cost_estimate=pl.CostEstimate(
            flops=2 * rows * (KEYW + LATENT), bytes_accessed=1 << 24, transcendentals=rows
        ),
    )(latents, rope_keys, cosine, sine, queries_nope, queries_rope, key_up, value_up, out_proj)


def solution(mesh):
    in_specs = (
        P("ctx", "head"),
        P("ctx", "head"),
        P("ctx", None),
        P("ctx", None),
        P("ctx"),
        P(None, "head"),
        P(None, "head"),
        P("head", "ctx"),
    )
    out_specs = P("ctx", "head")
    run = functools.partial(body, mesh.shape["ctx"], mesh.shape["head"])
    return jax.shard_map(run, mesh=mesh, in_specs=in_specs, out_specs=out_specs, check_vma=False)
```

```python
import functools
import math

import jax
import jax.numpy as jnp
from jax import lax
from jax.experimental import pallas as pl
from jax.experimental.pallas import tpu as pltpu
from jax.sharding import PartitionSpec as P

LATENT = 512
ROPE = 64
NOPE = 128
VDIM = 128
KEYW = 640
CORES = 2
LINES = 2
GROUP = 8
SPLIT = 2
CHUNKS = 4
LAG = 1

masked_value = -1e30
MESH = pl.DeviceIdType.MESH
NT = (((1,), (1,)), ((), ()))


def rope_tables(token_pos, width):
    half_width = width // 2
    freqs = jnp.exp(jnp.arange(half_width, dtype=jnp.float32) * (-2.0 * math.log(10000.0) / width))
    angle = token_pos.astype(jnp.float32)[:, None] * freqs[None, :]
    return (jnp.cos(angle), jnp.sin(angle))


def swap_halves(values):
    lane = lax.broadcasted_iota(jnp.int32, values.shape, 1)
    ahead = pltpu.roll(values, 2 * ROPE - ROPE // 2, 1)
    behind = pltpu.roll(values, ROPE // 2, 1)
    return jnp.where(lax.rem(lane, ROPE) < ROPE // 2, ahead, behind)


def kernel(
    n_ctx,
    n_head,
    lat_hbm,
    rk_hbm,
    cos_ref,
    sin_ref,
    qn_hbm,
    qr_hbm,
    key_up_hbm,
    value_up_hbm,
    proj_hbm,
    out_ref,
    lat_ref,
    rk_ref,
    wide,
    qn_ref,
    qr_ref,
    key_up,
    value_up,
    proj,
    kv,
    query,
    ho,
    acc,
    out_send,
    land,
    load_sem,
    proj_send_c,
    proj_send_y,
    proj_send_d,
    proj_recv_c,
    proj_recv_y,
    proj_recv_d,
    kv_send_z,
    kv_send_y,
    kv_send_c,
    kv_recv,
    ho_send_z,
    ho_recv,
    back_send,
    land_recv,
):
    tokens = lat_ref.shape[0]
    n_z = n_ctx // (CORES * LINES)
    sub = tokens // SPLIT
    ticks = ho.shape[0]
    groups = ticks // SPLIT
    depth = proj_hbm.shape[1]
    spots = land.shape[1]
    me = lax.axis_index("ctx")
    head = lax.axis_index("head")
    core = lax.rem(me, CORES)
    line = lax.rem(me // CORES, LINES)
    z = me // (CORES * LINES)
    other_line = 1 - line
    owner_head = z // spots
    slot = lax.rem(z, spots)

    def ctx_of(z_at, line_at, core_at):
        return (z_at * LINES + line_at) * CORES + core_at

    core_peer = (ctx_of(z, line, 1 - core), head)
    line_peer = (ctx_of(z, other_line, core), head)

    def z_peer(step):
        return lax.rem(z + step, n_z)

    barrier = pltpu.get_barrier_semaphore()
    n_class = (n_ctx // CORES) * n_head
    mine = (me // CORES) * n_head + head

    def greet(step, carry):
        other = lax.rem(mine + step, n_class)
        there = ((other // n_head) * CORES + core, lax.rem(other, n_head))
        pl.semaphore_signal(barrier, inc=1, device_id=there, device_id_type=MESH)
        return carry

    lax.fori_loop(1, n_class, greet, 0)
    pl.semaphore_signal(barrier, inc=1, device_id=core_peer, device_id_type=MESH)

    loads = []
    for source, target in (
        (lat_hbm, lat_ref),
        (rk_hbm, rk_ref),
        (qn_hbm, qn_ref),
        (qr_hbm, qr_ref),
        (key_up_hbm, key_up),
        (value_up_hbm, value_up),
        (proj_hbm, proj.at[line, core]),
    ):
        loads.append(pltpu.make_async_copy(source, target, load_sem.at[len(loads)]))
        loads[-1].start()
    load_lat, load_rk, load_qn, load_qr, load_key, load_value, load_proj = loads
    wide[...] = jnp.zeros_like(wide)
    load_lat.wait()
    load_rk.wait()
    wide[:, pl.ds(0, ROPE)] = rk_ref[...].astype(jnp.float32)
    pl.semaphore_wait(barrier, n_class)

    def kv_copy(src, origin, send_sem, there):
        return pltpu.make_async_remote_copy(
            src_ref=src,
            dst_ref=kv.at[origin],
            send_sem=send_sem,
            recv_sem=kv_recv.at[origin],
            device_id=there,
            device_id_type=MESH,
        )

    def rotated(values):
        values = values.astype(jnp.float32)
        return values * cos_ref[...] + swap_halves(values) * sin_ref[...]

    kv[me, :, pl.ds(0, LATENT)] = lat_ref[...]
    kv[me, :, pl.ds(LATENT, KEYW - LATENT)] = rotated(wide[...]).astype(jnp.bfloat16)

    sends = []

    def send_if(allowed, origin, send_sem, there):
        copy = kv_copy(kv.at[origin], origin, send_sem, there)
        sends.append((allowed, copy))
        if allowed is None:
            copy.start()
        else:
            pl.when(allowed)(copy.start)

    for step in range(1, n_z):
        there = (ctx_of(lax.rem(z + step, n_z), line, core), head)
        send_if(z + step < n_z, me, kv_send_z.at[step - 1], there)
    send_if(None, me, kv_send_y.at[0], line_peer)
    send_if(None, me, kv_send_c.at[0, 0], core_peer)
    for step in range(1, n_z):

        @pl.when(z + step < n_z)
        def _():
            later = pl.ds((z + step) * (LINES * CORES), LINES * CORES)
            kv[later] = jnp.zeros((LINES * CORES, tokens, KEYW), jnp.bfloat16)

    def chunk_of(index):
        return pl.ds(index * (depth // CHUNKS), depth // CHUNKS)

    proj_core = pltpu.make_async_remote_copy(
        src_ref=proj_hbm,
        dst_ref=proj.at[line, core],
        send_sem=proj_send_c,
        recv_sem=proj_recv_c,
        device_id=core_peer,
        device_id_type=MESH,
    )

    def proj_line(index):
        return pltpu.make_async_remote_copy(
            src_ref=proj_hbm.at[:, chunk_of(index)],
            dst_ref=proj.at[line, core, :, chunk_of(index)],
            send_sem=proj_send_y.at[index],
            recv_sem=proj_recv_y.at[index],
            device_id=line_peer,
            device_id_type=MESH,
        )

    def proj_across(index):
        return pltpu.make_async_remote_copy(
            src_ref=proj.at[other_line, core, :, chunk_of(index)],
            dst_ref=proj.at[other_line, core, :, chunk_of(index)],
            send_sem=proj_send_d.at[index],
            recv_sem=proj_recv_d.at[index],
            device_id=core_peer,
            device_id_type=MESH,
        )

    for index in range(CHUNKS):
        proj_line(index).start()

    load_qn.wait()
    load_qr.wait()
    load_key.wait()

    def up(group, carry):
        for part in range(GROUP):
            columns = pl.ds(pl.multiple_of((group * GROUP + part) * NOPE, NOPE), NOPE)
            made = lax.dot_general(
                qn_ref[:, columns], key_up[:, columns], NT, preferred_element_type=jnp.float32
            ).astype(jnp.bfloat16)
            for half in range(SPLIT):
                query[half * groups + group, pl.ds(part * sub, sub), pl.ds(0, LATENT)] = made[
                    half * sub : (half + 1) * sub
                ]
        for pair in range(GROUP // 2):
            start = pl.multiple_of((group * (GROUP // 2) + pair) * 2 * ROPE, 2 * ROPE)
            both = rotated(qr_ref[:, pl.ds(start, 2 * ROPE)])
            for part, turned in ((0, both), (1, pltpu.roll(both, ROPE, 1))):
                rows = pl.ds((2 * pair + part) * sub, sub)
                turned = turned.astype(jnp.bfloat16)
                for half in range(SPLIT):
                    query[half * groups + group, rows, pl.ds(LATENT, KEYW - LATENT)] = turned[
                        half * sub : (half + 1) * sub
                    ]
        return carry

    lax.fori_loop(0, groups, up, 0)

    def kv_wait(origin):
        kv_copy(kv.at[origin], origin, kv_send_y.at[0], line_peer).wait_recv()

    def earlier(step):
        return lax.rem(z + n_z - step, n_z)

    for step in range(1, n_z):
        origin = ctx_of(earlier(step), line, core)
        allowed = z >= step
        pl.when(allowed)(functools.partial(kv_wait, origin))
        send_if(allowed, origin, kv_send_y.at[step], line_peer)
        send_if(allowed, origin, kv_send_c.at[0, step], core_peer)
    for step in range(n_z):
        origin = ctx_of(earlier(step), other_line, core)
        allowed = z >= step
        pl.when(allowed)(functools.partial(kv_wait, origin))
        send_if(allowed, origin, kv_send_c.at[1, step], core_peer)
    proj_core.start()
    for step in range(n_z):
        for line_at in (line, other_line):
            origin = ctx_of(earlier(step), line_at, 1 - core)
            pl.when(z >= step)(functools.partial(kv_wait, origin))
    load_value.wait()

    above = z + 1 < n_z
    below = z >= 1
    up_peer = (ctx_of(lax.rem(z + 1, n_z), line, core), head)
    down_peer = (ctx_of(lax.rem(z + n_z - 1, n_z), line, core), head)

    def ho_copy(way, time, z_at, there):
        return pltpu.make_async_remote_copy(
            src_ref=ho.at[time, z_at],
            dst_ref=ho.at[time, z_at],
            send_sem=ho_send_z.at[way, time, z_at],
            recv_sem=ho_recv.at[time, z_at],
            device_id=there,
            device_id_type=MESH,
        )

    def up_copy(time, z_at):
        return ho_copy(0, time, z_at, up_peer)

    def down_copy(time, z_at):
        return ho_copy(1, time, z_at, down_peer)

    scale = math.log2(math.e) / math.sqrt(NOPE + ROPE)
    n_rows = GROUP * sub

    def attend(time, blocks):
        half = time // groups
        group = lax.rem(time, groups)
        n_keys = blocks * tokens
        keys = kv[pl.ds(0, blocks)].reshape(n_keys, KEYW)
        scores = lax.dot_general(query[time], keys, NT, preferred_element_type=jnp.float32)
        row = lax.broadcasted_iota(jnp.int32, (n_rows, 1), 0)
        last = me * tokens + half * sub + lax.rem(row, sub)
        key_index = lax.broadcasted_iota(jnp.int32, (n_rows, n_keys), 1)
        scores = jnp.where(key_index <= last, scores, masked_value)
        peak = jnp.max(scores, axis=1, keepdims=True)
        weights = jnp.exp2((scores - peak) * scale)
        totals = jnp.sum(weights, axis=1, keepdims=True)
        summed = jnp.dot(
            weights.astype(jnp.bfloat16), keys[:, :LATENT], preferred_element_type=jnp.float32
        )
        latent_out = (summed * (1.0 / totals)).astype(jnp.bfloat16)
        for part in range(GROUP):
            columns = pl.ds(pl.multiple_of((group * GROUP + part) * VDIM, VDIM), VDIM)
            ho[time, z, :, pl.ds(part * VDIM, VDIM)] = jnp.dot(
                latent_out[part * sub : (part + 1) * sub],
                value_up[:, columns],
                preferred_element_type=jnp.float32,
            ).astype(jnp.bfloat16)

    def tick(time, carry):
        @pl.when(time < ticks)
        def _():
            pl.when(2 * z < n_z)(functools.partial(attend, time, n_ctx // 2))
            pl.when(2 * z >= n_z)(functools.partial(attend, time, n_ctx))
            pl.when(above)(lambda: up_copy(time, z).start())
            pl.when(below)(lambda: down_copy(time, z).start())

        for step in range(1, n_z - 1):
            past = time - step - LAG
            in_time = jnp.logical_and(past >= 0, past < ticks)

            @pl.when(jnp.logical_and(in_time, jnp.logical_and(z >= step, above)))
            def _():
                up_copy(past, z - step).wait_recv()
                up_copy(past, z - step).start()

            @pl.when(jnp.logical_and(in_time, jnp.logical_and(z + step < n_z, below)))
            def _():
                down_copy(past, z + step).wait_recv()
                down_copy(past, z + step).start()

        return carry

    lax.fori_loop(0, ticks + n_z - 2 + LAG, tick, 0)

    for index in range(CHUNKS):
        proj_line(index).wait_recv()
        proj_across(index).start()
    load_proj.wait()
    proj_core.wait_recv()
    for index in range(CHUNKS):
        proj_across(index).wait_recv()

    def back(half, z_at):
        return pltpu.make_async_remote_copy(
            src_ref=out_send.at[half, z_at],
            dst_ref=land.at[head, slot, half],
            send_sem=back_send.at[half, z_at],
            recv_sem=land_recv.at[head, slot, half],
            device_id=(ctx_of(z_at, line, core), owner_head),
            device_id_type=MESH,
        )

    stays = owner_head == head

    for half in range(SPLIT):
        acc[...] = jnp.zeros_like(acc)

        def add(group, carry):
            time = half * groups + group
            for step in range(1, n_z):

                @pl.when(jnp.logical_and(z >= step, jnp.logical_or(z == n_z - 1, step == n_z - 1)))
                def _():
                    up_copy(time, z - step).wait_recv()

                @pl.when(jnp.logical_and(z + step < n_z, jnp.logical_or(z == 0, step == n_z - 1)))
                def _():
                    down_copy(time, z + step).wait_recv()

            block = ho[time].reshape(n_z * sub, GROUP * VDIM)
            span = pl.ds(pl.multiple_of(group * (GROUP * VDIM), GROUP * VDIM), GROUP * VDIM)
            for line_at in range(LINES):
                for core_at in range(CORES):
                    acc[line_at, core_at] += lax.dot_general(
                        block,
                        proj[line_at, core_at, :, span],
                        NT,
                        preferred_element_type=jnp.float32,
                    )
            return carry

        lax.fori_loop(0, groups, add, 0)
        for z_at in range(n_z):
            out_send[half, z_at] = acc[:, :, pl.ds(z_at * sub, sub), :].astype(jnp.bfloat16)
        for step in range(1, n_z):
            back(half, z_peer(step)).start()

        @pl.when(stays)
        def _():
            pltpu.make_async_copy(
                out_send.at[half, z], land.at[head, slot, half], land_recv.at[head, slot, half]
            ).start()

        @pl.when(jnp.logical_not(stays))
        def _():
            back(half, z).start()

    for half in range(SPLIT):
        for part in range(n_head):
            for spot in range(spots):
                pltpu.make_async_copy(
                    out_send.at[0, 0], land.at[part, spot, half], land_recv.at[part, spot, half]
                ).wait()
        columns = []
        for spot in range(spots):
            for line_at in range(LINES):
                for core_at in range(CORES):
                    total = land[0, spot, half, line_at, core_at].astype(jnp.float32)
                    for part in range(1, n_head):
                        total += land[part, spot, half, line_at, core_at].astype(jnp.float32)
                    columns.append(total)
        out_ref[pl.ds(half * sub, sub), :] = jnp.concatenate(columns, axis=1).astype(out_ref.dtype)

    for allowed, copy in sends:
        if allowed is None:
            copy.wait_send()
        else:
            pl.when(allowed)(copy.wait_send)
    proj_core.wait_send()
    for index in range(CHUNKS):
        proj_line(index).wait_send()
        proj_across(index).wait_send()

    def drain(time, carry):
        for z_at in range(n_z):
            pl.when(jnp.logical_and(above, z >= z_at))(up_copy(time, z_at).wait_send)
            pl.when(jnp.logical_and(below, z <= z_at))(down_copy(time, z_at).wait_send)
        return carry

    lax.fori_loop(0, ticks, drain, 0)
    for half in range(SPLIT):
        for step in range(1, n_z):
            back(half, z_peer(step)).wait_send()
        pl.when(jnp.logical_not(stays))(back(half, z).wait_send)


def body(
    n_ctx,
    n_head,
    queries_nope,
    queries_rope,
    latents,
    rope_keys,
    positions,
    key_up,
    value_up,
    out_proj,
):
    tokens = latents.shape[0]
    heads = key_up.shape[1] // NOPE
    groups = heads // GROUP
    n_z = n_ctx // (CORES * LINES)
    spots = n_z // n_head
    sub = tokens // SPLIT
    width = out_proj.shape[1]
    bf16 = jnp.bfloat16
    cosine, sine = rope_tables(positions, ROPE)
    cosine = jnp.concatenate([cosine] * 4, axis=1)
    sine = jnp.concatenate([-sine, sine] * 2, axis=1)
    out_proj = out_proj.T
    vmem = pl.BlockSpec(memory_space=pltpu.VMEM)
    hbm = pl.BlockSpec(memory_space=pltpu.HBM)
    dma = pltpu.SemaphoreType.DMA
    rows = n_ctx * tokens * heads * tokens
    return pl.pallas_call(
        functools.partial(kernel, n_ctx, n_head),
        out_shape=jax.ShapeDtypeStruct((tokens, spots * LINES * CORES * width), bf16),
        in_specs=[hbm] * 2 + [vmem] * 2 + [hbm] * 5,
        out_specs=vmem,
        scratch_shapes=[
            pltpu.VMEM(latents.shape, bf16),
            pltpu.VMEM(rope_keys.shape, bf16),
            pltpu.VMEM((tokens, KEYW - LATENT), jnp.float32),
            pltpu.VMEM(queries_nope.shape, bf16),
            pltpu.VMEM(queries_rope.shape, bf16),
            pltpu.VMEM(key_up.shape, bf16),
            pltpu.VMEM(value_up.shape, bf16),
            pltpu.VMEM((LINES, CORES) + out_proj.shape, bf16),
            pltpu.VMEM((n_ctx, tokens, KEYW), bf16),
            pltpu.VMEM((SPLIT * groups, GROUP * sub, KEYW), bf16),
            pltpu.VMEM((SPLIT * groups, n_z, sub, GROUP * VDIM), bf16),
            pltpu.VMEM((LINES, CORES, n_z * sub, width), jnp.float32),
            pltpu.VMEM((SPLIT, n_z, LINES, CORES, sub, width), bf16),
            pltpu.VMEM((n_head, spots, SPLIT, LINES, CORES, sub, width), bf16),
            dma((7,)),
            dma,
            dma((CHUNKS,)),
            dma((CHUNKS,)),
            dma,
            dma((CHUNKS,)),
            dma((CHUNKS,)),
            dma((n_z,)),
            dma((n_z,)),
            dma((LINES, n_z)),
            dma((n_ctx,)),
            dma((2, SPLIT * groups, n_z)),
            dma((SPLIT * groups, n_z)),
            dma((SPLIT, n_z)),
            dma((n_head, spots, SPLIT)),
        ],
        compiler_params=pltpu.CompilerParams(
            collective_id=0, has_side_effects=True, vmem_limit_bytes=52 * 1024 * 1024
        ),
        cost_estimate=pl.CostEstimate(
            flops=2 * rows * (KEYW + LATENT), bytes_accessed=1 << 24, transcendentals=rows
        ),
    )(latents, rope_keys, cosine, sine, queries_nope, queries_rope, key_up, value_up, out_proj)


def solution(mesh):
    in_specs = (
        P("ctx", "head"),
        P("ctx", "head"),
        P("ctx", None),
        P("ctx", None),
        P("ctx"),
        P(None, "head"),
        P(None, "head"),
        P("head", "ctx"),
    )
    out_specs = P("ctx", "head")
    run = functools.partial(body, mesh.shape["ctx"], mesh.shape["head"])
    return jax.shard_map(run, mesh=mesh, in_specs=in_specs, out_specs=out_specs, check_vma=False)
```

```python
import functools
import math

import jax
import jax.numpy as jnp
from jax import lax
from jax.experimental import pallas as pl
from jax.experimental.pallas import tpu as pltpu
from jax.sharding import PartitionSpec as P

LATENT = 512
ROPE = 64
NOPE = 128
VDIM = 128
KEYW = 640
CORES = 2
LINES = 2
GROUP = 8
SPLIT = 2
CHUNKS = 8
LAG = 1

masked_value = -1e30
MESH = pl.DeviceIdType.MESH
NT = (((1,), (1,)), ((), ()))


def rope_tables(token_pos, width):
    half_width = width // 2
    freqs = jnp.exp(jnp.arange(half_width, dtype=jnp.float32) * (-2.0 * math.log(10000.0) / width))
    angle = token_pos.astype(jnp.float32)[:, None] * freqs[None, :]
    return (jnp.cos(angle), jnp.sin(angle))


def swap_halves(values):
    lane = lax.broadcasted_iota(jnp.int32, values.shape, 1)
    ahead = pltpu.roll(values, 2 * ROPE - ROPE // 2, 1)
    behind = pltpu.roll(values, ROPE // 2, 1)
    return jnp.where(lax.rem(lane, ROPE) < ROPE // 2, ahead, behind)


def kernel(
    n_ctx,
    n_head,
    lat_hbm,
    rk_hbm,
    cos_ref,
    sin_ref,
    qn_hbm,
    qr_hbm,
    key_up_hbm,
    value_up_hbm,
    proj_hbm,
    out_ref,
    lat_ref,
    rk_ref,
    wide,
    qn_ref,
    qr_ref,
    key_up,
    value_up,
    proj,
    kv,
    query,
    ho,
    acc,
    out_send,
    land,
    load_sem,
    proj_send_c,
    proj_send_y,
    proj_send_d,
    proj_recv_c,
    proj_recv_y,
    proj_recv_d,
    kv_send_z,
    kv_send_y,
    kv_send_c,
    kv_recv,
    ho_send_z,
    ho_recv,
    back_send,
    land_recv,
):
    tokens = lat_ref.shape[0]
    n_z = n_ctx // (CORES * LINES)
    sub = tokens // SPLIT
    ticks = ho.shape[0]
    groups = ticks // SPLIT
    depth = proj_hbm.shape[1]
    spots = land.shape[1]
    me = lax.axis_index("ctx")
    head = lax.axis_index("head")
    core = lax.rem(me, CORES)
    line = lax.rem(me // CORES, LINES)
    z = me // (CORES * LINES)
    other_line = 1 - line
    owner_head = z // spots
    slot = lax.rem(z, spots)

    def ctx_of(z_at, line_at, core_at):
        return (z_at * LINES + line_at) * CORES + core_at

    core_peer = (ctx_of(z, line, 1 - core), head)
    line_peer = (ctx_of(z, other_line, core), head)

    def z_peer(step):
        return lax.rem(z + step, n_z)

    barrier = pltpu.get_barrier_semaphore()
    n_class = (n_ctx // CORES) * n_head
    mine = (me // CORES) * n_head + head

    def greet(step, carry):
        other = lax.rem(mine + step, n_class)
        there = ((other // n_head) * CORES + core, lax.rem(other, n_head))
        pl.semaphore_signal(barrier, inc=1, device_id=there, device_id_type=MESH)
        return carry

    lax.fori_loop(1, n_class, greet, 0)
    pl.semaphore_signal(barrier, inc=1, device_id=core_peer, device_id_type=MESH)

    loads = []
    for source, target in (
        (lat_hbm, lat_ref),
        (rk_hbm, rk_ref),
        (qn_hbm, qn_ref),
        (qr_hbm, qr_ref),
        (key_up_hbm, key_up),
        (value_up_hbm, value_up),
        (proj_hbm, proj.at[line, core]),
    ):
        loads.append(pltpu.make_async_copy(source, target, load_sem.at[len(loads)]))
        loads[-1].start()
    load_lat, load_rk, load_qn, load_qr, load_key, load_value, load_proj = loads
    wide[...] = jnp.zeros_like(wide)
    load_lat.wait()
    load_rk.wait()
    wide[:, pl.ds(0, ROPE)] = rk_ref[...].astype(jnp.float32)
    pl.semaphore_wait(barrier, n_class)

    def kv_copy(src, origin, send_sem, there):
        return pltpu.make_async_remote_copy(
            src_ref=src,
            dst_ref=kv.at[origin],
            send_sem=send_sem,
            recv_sem=kv_recv.at[origin],
            device_id=there,
            device_id_type=MESH,
        )

    def rotated(values):
        values = values.astype(jnp.float32)
        return values * cos_ref[...] + swap_halves(values) * sin_ref[...]

    kv[me, :, pl.ds(0, LATENT)] = lat_ref[...]
    kv[me, :, pl.ds(LATENT, KEYW - LATENT)] = rotated(wide[...]).astype(jnp.bfloat16)

    sends = []

    def send_if(allowed, origin, send_sem, there):
        copy = kv_copy(kv.at[origin], origin, send_sem, there)
        sends.append((allowed, copy))
        if allowed is None:
            copy.start()
        else:
            pl.when(allowed)(copy.start)

    for step in range(1, n_z):
        there = (ctx_of(lax.rem(z + step, n_z), line, core), head)
        send_if(z + step < n_z, me, kv_send_z.at[step - 1], there)
    send_if(None, me, kv_send_y.at[0], line_peer)
    send_if(None, me, kv_send_c.at[0, 0], core_peer)
    for step in range(1, n_z):

        @pl.when(z + step < n_z)
        def _():
            later = pl.ds((z + step) * (LINES * CORES), LINES * CORES)
            kv[later] = jnp.zeros((LINES * CORES, tokens, KEYW), jnp.bfloat16)

    def chunk_of(index):
        width = depth // CHUNKS
        return pl.ds(pl.multiple_of(index * width, width), width)

    proj_core = pltpu.make_async_remote_copy(
        src_ref=proj_hbm,
        dst_ref=proj.at[line, core],
        send_sem=proj_send_c,
        recv_sem=proj_recv_c,
        device_id=core_peer,
        device_id_type=MESH,
    )

    def proj_line(index):
        return pltpu.make_async_remote_copy(
            src_ref=proj_hbm.at[:, chunk_of(index)],
            dst_ref=proj.at[line, core, :, chunk_of(index)],
            send_sem=proj_send_y.at[index],
            recv_sem=proj_recv_y.at[index],
            device_id=line_peer,
            device_id_type=MESH,
        )

    def proj_across(index):
        return pltpu.make_async_remote_copy(
            src_ref=proj.at[other_line, core, :, chunk_of(index)],
            dst_ref=proj.at[other_line, core, :, chunk_of(index)],
            send_sem=proj_send_d.at[index],
            recv_sem=proj_recv_d.at[index],
            device_id=core_peer,
            device_id_type=MESH,
        )

    load_qn.wait()
    load_qr.wait()
    load_key.wait()

    def up(group, carry):
        for part in range(GROUP):
            columns = pl.ds(pl.multiple_of((group * GROUP + part) * NOPE, NOPE), NOPE)
            made = lax.dot_general(
                qn_ref[:, columns], key_up[:, columns], NT, preferred_element_type=jnp.float32
            ).astype(jnp.bfloat16)
            for half in range(SPLIT):
                query[half * groups + group, pl.ds(part * sub, sub), pl.ds(0, LATENT)] = made[
                    half * sub : (half + 1) * sub
                ]
        for pair in range(GROUP // 2):
            start = pl.multiple_of((group * (GROUP // 2) + pair) * 2 * ROPE, 2 * ROPE)
            both = rotated(qr_ref[:, pl.ds(start, 2 * ROPE)])
            for part, turned in ((0, both), (1, pltpu.roll(both, ROPE, 1))):
                rows = pl.ds((2 * pair + part) * sub, sub)
                turned = turned.astype(jnp.bfloat16)
                for half in range(SPLIT):
                    query[half * groups + group, rows, pl.ds(LATENT, KEYW - LATENT)] = turned[
                        half * sub : (half + 1) * sub
                    ]
        return carry

    lax.fori_loop(0, groups, up, 0)

    def kv_wait(origin):
        kv_copy(kv.at[origin], origin, kv_send_y.at[0], line_peer).wait_recv()

    def earlier(step):
        return lax.rem(z + n_z - step, n_z)

    for step in range(1, n_z):
        origin = ctx_of(earlier(step), line, core)
        allowed = z >= step
        pl.when(allowed)(functools.partial(kv_wait, origin))
        send_if(allowed, origin, kv_send_y.at[step], line_peer)
        send_if(allowed, origin, kv_send_c.at[0, step], core_peer)
    for step in range(n_z):
        origin = ctx_of(earlier(step), other_line, core)
        allowed = z >= step
        pl.when(allowed)(functools.partial(kv_wait, origin))
        send_if(allowed, origin, kv_send_c.at[1, step], core_peer)
    proj_core.start()
    for step in range(n_z):
        for line_at in (line, other_line):
            origin = ctx_of(earlier(step), line_at, 1 - core)
            pl.when(z >= step)(functools.partial(kv_wait, origin))
    load_value.wait()

    above = z + 1 < n_z
    below = z >= 1
    up_peer = (ctx_of(lax.rem(z + 1, n_z), line, core), head)
    down_peer = (ctx_of(lax.rem(z + n_z - 1, n_z), line, core), head)

    def ho_copy(way, time, z_at, there):
        return pltpu.make_async_remote_copy(
            src_ref=ho.at[time, z_at],
            dst_ref=ho.at[time, z_at],
            send_sem=ho_send_z.at[way, time, z_at],
            recv_sem=ho_recv.at[time, z_at],
            device_id=there,
            device_id_type=MESH,
        )

    def up_copy(time, z_at):
        return ho_copy(0, time, z_at, up_peer)

    def down_copy(time, z_at):
        return ho_copy(1, time, z_at, down_peer)

    scale = math.log2(math.e) / math.sqrt(NOPE + ROPE)
    n_rows = GROUP * sub

    def attend(time, blocks):
        half = time // groups
        group = lax.rem(time, groups)
        n_keys = blocks * tokens
        keys = kv[pl.ds(0, blocks)].reshape(n_keys, KEYW)
        scores = lax.dot_general(query[time], keys, NT, preferred_element_type=jnp.float32)
        row = lax.broadcasted_iota(jnp.int32, (n_rows, 1), 0)
        last = me * tokens + half * sub + lax.rem(row, sub)
        key_index = lax.broadcasted_iota(jnp.int32, (n_rows, n_keys), 1)
        scores = jnp.where(key_index <= last, scores, masked_value)
        peak = jnp.max(scores, axis=1, keepdims=True)
        weights = jnp.exp2((scores - peak) * scale)
        totals = jnp.sum(weights, axis=1, keepdims=True)
        summed = jnp.dot(
            weights.astype(jnp.bfloat16), keys[:, :LATENT], preferred_element_type=jnp.float32
        )
        latent_out = (summed * (1.0 / totals)).astype(jnp.bfloat16)
        for part in range(GROUP):
            columns = pl.ds(pl.multiple_of((group * GROUP + part) * VDIM, VDIM), VDIM)
            ho[time, z, :, pl.ds(part * VDIM, VDIM)] = jnp.dot(
                latent_out[part * sub : (part + 1) * sub],
                value_up[:, columns],
                preferred_element_type=jnp.float32,
            ).astype(jnp.bfloat16)

    def tick(time, carry):
        pl.when(time < CHUNKS)(lambda: proj_line(time).start())

        @pl.when(time < ticks)
        def _():
            pl.when(2 * z < n_z)(functools.partial(attend, time, n_ctx // 2))
            pl.when(2 * z >= n_z)(functools.partial(attend, time, n_ctx))
            pl.when(above)(lambda: up_copy(time, z).start())
            pl.when(below)(lambda: down_copy(time, z).start())

        for step in range(1, n_z - 1):
            past = time - step - LAG
            in_time = jnp.logical_and(past >= 0, past < ticks)

            @pl.when(jnp.logical_and(in_time, jnp.logical_and(z >= step, above)))
            def _():
                up_copy(past, z - step).wait_recv()
                up_copy(past, z - step).start()

            @pl.when(jnp.logical_and(in_time, jnp.logical_and(z + step < n_z, below)))
            def _():
                down_copy(past, z + step).wait_recv()
                down_copy(past, z + step).start()

        return carry

    lax.fori_loop(0, max(ticks + n_z - 2 + LAG, CHUNKS), tick, 0)

    for index in range(CHUNKS):
        proj_line(index).wait_recv()
        proj_across(index).start()
    load_proj.wait()
    proj_core.wait_recv()
    for index in range(CHUNKS):
        proj_across(index).wait_recv()

    def back(half, z_at):
        return pltpu.make_async_remote_copy(
            src_ref=out_send.at[half, z_at],
            dst_ref=land.at[head, slot, half],
            send_sem=back_send.at[half, z_at],
            recv_sem=land_recv.at[head, slot, half],
            device_id=(ctx_of(z_at, line, core), owner_head),
            device_id_type=MESH,
        )

    stays = owner_head == head

    for half in range(SPLIT):
        acc[...] = jnp.zeros_like(acc)

        def add(group, carry):
            time = half * groups + group
            for step in range(1, n_z):

                @pl.when(jnp.logical_and(z >= step, jnp.logical_or(z == n_z - 1, step == n_z - 1)))
                def _():
                    up_copy(time, z - step).wait_recv()

                @pl.when(jnp.logical_and(z + step < n_z, jnp.logical_or(z == 0, step == n_z - 1)))
                def _():
                    down_copy(time, z + step).wait_recv()

            block = ho[time].reshape(n_z * sub, GROUP * VDIM)
            span = pl.ds(pl.multiple_of(group * (GROUP * VDIM), GROUP * VDIM), GROUP * VDIM)
            for line_at in range(LINES):
                for core_at in range(CORES):
                    acc[line_at, core_at] += lax.dot_general(
                        block,
                        proj[line_at, core_at, :, span],
                        NT,
                        preferred_element_type=jnp.float32,
                    )
            return carry

        lax.fori_loop(0, groups, add, 0)
        for z_at in range(n_z):
            out_send[half, z_at] = acc[:, :, pl.ds(z_at * sub, sub), :].astype(jnp.bfloat16)
        for step in range(1, n_z):
            back(half, z_peer(step)).start()

        @pl.when(stays)
        def _():
            pltpu.make_async_copy(
                out_send.at[half, z], land.at[head, slot, half], land_recv.at[head, slot, half]
            ).start()

        @pl.when(jnp.logical_not(stays))
        def _():
            back(half, z).start()

    for half in range(SPLIT):
        for part in range(n_head):
            for spot in range(spots):
                pltpu.make_async_copy(
                    out_send.at[0, 0], land.at[part, spot, half], land_recv.at[part, spot, half]
                ).wait()
        columns = []
        for spot in range(spots):
            for line_at in range(LINES):
                for core_at in range(CORES):
                    total = land[0, spot, half, line_at, core_at].astype(jnp.float32)
                    for part in range(1, n_head):
                        total += land[part, spot, half, line_at, core_at].astype(jnp.float32)
                    columns.append(total)
        out_ref[pl.ds(half * sub, sub), :] = jnp.concatenate(columns, axis=1).astype(out_ref.dtype)

    for allowed, copy in sends:
        if allowed is None:
            copy.wait_send()
        else:
            pl.when(allowed)(copy.wait_send)
    proj_core.wait_send()
    for index in range(CHUNKS):
        proj_line(index).wait_send()
        proj_across(index).wait_send()

    def drain(time, carry):
        for z_at in range(n_z):
            pl.when(jnp.logical_and(above, z >= z_at))(up_copy(time, z_at).wait_send)
            pl.when(jnp.logical_and(below, z <= z_at))(down_copy(time, z_at).wait_send)
        return carry

    lax.fori_loop(0, ticks, drain, 0)
    for half in range(SPLIT):
        for step in range(1, n_z):
            back(half, z_peer(step)).wait_send()
        pl.when(jnp.logical_not(stays))(back(half, z).wait_send)


def body(
    n_ctx,
    n_head,
    queries_nope,
    queries_rope,
    latents,
    rope_keys,
    positions,
    key_up,
    value_up,
    out_proj,
):
    tokens = latents.shape[0]
    heads = key_up.shape[1] // NOPE
    groups = heads // GROUP
    n_z = n_ctx // (CORES * LINES)
    spots = n_z // n_head
    sub = tokens // SPLIT
    width = out_proj.shape[1]
    bf16 = jnp.bfloat16
    cosine, sine = rope_tables(positions, ROPE)
    cosine = jnp.concatenate([cosine] * 4, axis=1)
    sine = jnp.concatenate([-sine, sine] * 2, axis=1)
    out_proj = out_proj.T
    vmem = pl.BlockSpec(memory_space=pltpu.VMEM)
    hbm = pl.BlockSpec(memory_space=pl.ANY)
    dma = pltpu.SemaphoreType.DMA
    rows = n_ctx * tokens * heads * tokens
    return pl.pallas_call(
        functools.partial(kernel, n_ctx, n_head),
        out_shape=jax.ShapeDtypeStruct((tokens, spots * LINES * CORES * width), bf16),
        in_specs=[hbm] * 2 + [vmem] * 2 + [hbm] * 5,
        out_specs=vmem,
        scratch_shapes=[
            pltpu.VMEM(latents.shape, bf16),
            pltpu.VMEM(rope_keys.shape, bf16),
            pltpu.VMEM((tokens, KEYW - LATENT), jnp.float32),
            pltpu.VMEM(queries_nope.shape, bf16),
            pltpu.VMEM(queries_rope.shape, bf16),
            pltpu.VMEM(key_up.shape, bf16),
            pltpu.VMEM(value_up.shape, bf16),
            pltpu.VMEM((LINES, CORES) + out_proj.shape, bf16),
            pltpu.VMEM((n_ctx, tokens, KEYW), bf16),
            pltpu.VMEM((SPLIT * groups, GROUP * sub, KEYW), bf16),
            pltpu.VMEM((SPLIT * groups, n_z, sub, GROUP * VDIM), bf16),
            pltpu.VMEM((LINES, CORES, n_z * sub, width), jnp.float32),
            pltpu.VMEM((SPLIT, n_z, LINES, CORES, sub, width), bf16),
            pltpu.VMEM((n_head, spots, SPLIT, LINES, CORES, sub, width), bf16),
            dma((7,)),
            dma,
            dma((CHUNKS,)),
            dma((CHUNKS,)),
            dma,
            dma((CHUNKS,)),
            dma((CHUNKS,)),
            dma((n_z,)),
            dma((n_z,)),
            dma((LINES, n_z)),
            dma((n_ctx,)),
            dma((2, SPLIT * groups, n_z)),
            dma((SPLIT * groups, n_z)),
            dma((SPLIT, n_z)),
            dma((n_head, spots, SPLIT)),
        ],
        compiler_params=pltpu.CompilerParams(
            collective_id=0, has_side_effects=True, vmem_limit_bytes=52 * 1024 * 1024
        ),
        cost_estimate=pl.CostEstimate(
            flops=2 * rows * (KEYW + LATENT), bytes_accessed=1 << 24, transcendentals=rows
        ),
    )(latents, rope_keys, cosine, sine, queries_nope, queries_rope, key_up, value_up, out_proj)


def solution(mesh):
    in_specs = (
        P("ctx", "head"),
        P("ctx", "head"),
        P("ctx", None),
        P("ctx", None),
        P("ctx"),
        P(None, "head"),
        P(None, "head"),
        P("head", "ctx"),
    )
    out_specs = P("ctx", "head")
    run = functools.partial(body, mesh.shape["ctx"], mesh.shape["head"])
    return jax.shard_map(run, mesh=mesh, in_specs=in_specs, out_specs=out_specs, check_vma=False)
```

```python
import functools
import math

import jax
import jax.numpy as jnp
from jax import lax
from jax.experimental import pallas as pl
from jax.experimental.pallas import tpu as pltpu
from jax.sharding import PartitionSpec as P

LATENT = 512
ROPE = 64
NOPE = 128
VDIM = 128
KEYW = 640
CORES = 2
LINES = 2
GROUP = 8
SPLIT = 2
CHUNKS = 4
LAG = 1

masked_value = -1e30
MESH = pl.DeviceIdType.MESH
NT = (((1,), (1,)), ((), ()))


def rope_tables(token_pos, width):
    half_width = width // 2
    freqs = jnp.exp(jnp.arange(half_width, dtype=jnp.float32) * (-2.0 * math.log(10000.0) / width))
    angle = token_pos.astype(jnp.float32)[:, None] * freqs[None, :]
    return (jnp.cos(angle), jnp.sin(angle))


def swap_halves(values):
    lane = lax.broadcasted_iota(jnp.int32, values.shape, 1)
    ahead = pltpu.roll(values, 2 * ROPE - ROPE // 2, 1)
    behind = pltpu.roll(values, ROPE // 2, 1)
    return jnp.where(lax.rem(lane, ROPE) < ROPE // 2, ahead, behind)


def kernel(
    n_ctx,
    n_head,
    lat_hbm,
    rk_hbm,
    cos_ref,
    sin_ref,
    qn_hbm,
    qr_hbm,
    key_up_hbm,
    value_up_hbm,
    proj_hbm,
    out_ref,
    lat_ref,
    rk_ref,
    wide,
    qn_ref,
    qr_ref,
    key_up,
    value_up,
    proj,
    kv,
    query,
    ho,
    acc,
    out_send,
    land,
    load_sem,
    proj_send_c,
    proj_send_y,
    proj_send_d,
    proj_recv_c,
    proj_recv_y,
    proj_recv_d,
    kv_send_z,
    kv_send_y,
    kv_send_c,
    kv_recv,
    ho_send_z,
    ho_recv,
    back_send,
    land_recv,
):
    tokens = lat_ref.shape[0]
    n_z = n_ctx // (CORES * LINES)
    sub = tokens // SPLIT
    ticks = ho.shape[0]
    groups = ticks // SPLIT
    depth = proj_hbm.shape[1]
    spots = land.shape[1]
    me = lax.axis_index("ctx")
    head = lax.axis_index("head")
    core = lax.rem(me, CORES)
    line = lax.rem(me // CORES, LINES)
    z = me // (CORES * LINES)
    other_line = 1 - line
    owner_head = z // spots
    slot = lax.rem(z, spots)

    def ctx_of(z_at, line_at, core_at):
        return (z_at * LINES + line_at) * CORES + core_at

    core_peer = (ctx_of(z, line, 1 - core), head)
    line_peer = (ctx_of(z, other_line, core), head)

    def z_peer(step):
        return lax.rem(z + step, n_z)

    barrier = pltpu.get_barrier_semaphore()
    n_class = (n_ctx // CORES) * n_head
    mine = (me // CORES) * n_head + head

    def greet(step, carry):
        other = lax.rem(mine + step, n_class)
        there = ((other // n_head) * CORES + core, lax.rem(other, n_head))
        pl.semaphore_signal(barrier, inc=1, device_id=there, device_id_type=MESH)
        return carry

    lax.fori_loop(1, n_class, greet, 0)
    pl.semaphore_signal(barrier, inc=1, device_id=core_peer, device_id_type=MESH)

    loads = []
    for source, target in (
        (lat_hbm, lat_ref),
        (rk_hbm, rk_ref),
        (qn_hbm, qn_ref),
        (qr_hbm, qr_ref),
        (key_up_hbm, key_up),
        (value_up_hbm, value_up),
        (proj_hbm, proj.at[line, core]),
    ):
        loads.append(pltpu.make_async_copy(source, target, load_sem.at[len(loads)]))
        loads[-1].start()
    load_lat, load_rk, load_qn, load_qr, load_key, load_value, load_proj = loads
    wide[...] = jnp.zeros_like(wide)
    load_lat.wait()
    load_rk.wait()
    wide[:, pl.ds(0, ROPE)] = rk_ref[...].astype(jnp.float32)
    pl.semaphore_wait(barrier, n_class)

    def kv_copy(src, origin, send_sem, there):
        return pltpu.make_async_remote_copy(
            src_ref=src,
            dst_ref=kv.at[origin],
            send_sem=send_sem,
            recv_sem=kv_recv.at[origin],
            device_id=there,
            device_id_type=MESH,
        )

    def rotated(values):
        values = values.astype(jnp.float32)
        return values * cos_ref[...] + swap_halves(values) * sin_ref[...]

    kv[me, :, pl.ds(0, LATENT)] = lat_ref[...]
    kv[me, :, pl.ds(LATENT, KEYW - LATENT)] = rotated(wide[...]).astype(jnp.bfloat16)

    sends = []

    def send_if(allowed, origin, send_sem, there):
        copy = kv_copy(kv.at[origin], origin, send_sem, there)
        sends.append((allowed, copy))
        if allowed is None:
            copy.start()
        else:
            pl.when(allowed)(copy.start)

    for step in range(1, n_z):
        there = (ctx_of(lax.rem(z + step, n_z), line, core), head)
        send_if(z + step < n_z, me, kv_send_z.at[step - 1], there)
    send_if(None, me, kv_send_y.at[0], line_peer)
    send_if(None, me, kv_send_c.at[0, 0], core_peer)
    for step in range(1, n_z):

        @pl.when(z + step < n_z)
        def _():
            later = pl.ds((z + step) * (LINES * CORES), LINES * CORES)
            kv[later] = jnp.zeros((LINES * CORES, tokens, KEYW), jnp.bfloat16)

    def chunk_of(index):
        return pl.ds(index * (depth // CHUNKS), depth // CHUNKS)

    proj_core = pltpu.make_async_remote_copy(
        src_ref=proj_hbm,
        dst_ref=proj.at[line, core],
        send_sem=proj_send_c,
        recv_sem=proj_recv_c,
        device_id=core_peer,
        device_id_type=MESH,
    )

    def proj_line(index):
        return pltpu.make_async_remote_copy(
            src_ref=proj_hbm.at[:, chunk_of(index)],
            dst_ref=proj.at[line, core, :, chunk_of(index)],
            send_sem=proj_send_y.at[index],
            recv_sem=proj_recv_y.at[index],
            device_id=line_peer,
            device_id_type=MESH,
        )

    def proj_across(index):
        return pltpu.make_async_remote_copy(
            src_ref=proj.at[other_line, core, :, chunk_of(index)],
            dst_ref=proj.at[other_line, core, :, chunk_of(index)],
            send_sem=proj_send_d.at[index],
            recv_sem=proj_recv_d.at[index],
            device_id=core_peer,
            device_id_type=MESH,
        )

    load_qn.wait()
    load_qr.wait()
    load_key.wait()

    def up(group, carry):
        for part in range(GROUP):
            columns = pl.ds(pl.multiple_of((group * GROUP + part) * NOPE, NOPE), NOPE)
            made = lax.dot_general(
                qn_ref[:, columns], key_up[:, columns], NT, preferred_element_type=jnp.float32
            ).astype(jnp.bfloat16)
            for half in range(SPLIT):
                query[half * groups + group, pl.ds(part * sub, sub), pl.ds(0, LATENT)] = made[
                    half * sub : (half + 1) * sub
                ]
        for pair in range(GROUP // 2):
            start = pl.multiple_of((group * (GROUP // 2) + pair) * 2 * ROPE, 2 * ROPE)
            both = rotated(qr_ref[:, pl.ds(start, 2 * ROPE)])
            for part, turned in ((0, both), (1, pltpu.roll(both, ROPE, 1))):
                rows = pl.ds((2 * pair + part) * sub, sub)
                turned = turned.astype(jnp.bfloat16)
                for half in range(SPLIT):
                    query[half * groups + group, rows, pl.ds(LATENT, KEYW - LATENT)] = turned[
                        half * sub : (half + 1) * sub
                    ]
        return carry

    lax.fori_loop(0, groups, up, 0)

    def kv_wait(origin):
        kv_copy(kv.at[origin], origin, kv_send_y.at[0], line_peer).wait_recv()

    def earlier(step):
        return lax.rem(z + n_z - step, n_z)

    for step in range(1, n_z):
        origin = ctx_of(earlier(step), line, core)
        allowed = z >= step
        pl.when(allowed)(functools.partial(kv_wait, origin))
        send_if(allowed, origin, kv_send_y.at[step], line_peer)
        send_if(allowed, origin, kv_send_c.at[0, step], core_peer)
    for index in range(CHUNKS):
        proj_line(index).start()
    for step in range(n_z):
        origin = ctx_of(earlier(step), other_line, core)
        allowed = z >= step
        pl.when(allowed)(functools.partial(kv_wait, origin))
        send_if(allowed, origin, kv_send_c.at[1, step], core_peer)
    proj_core.start()
    for step in range(n_z):
        for line_at in (line, other_line):
            origin = ctx_of(earlier(step), line_at, 1 - core)
            pl.when(z >= step)(functools.partial(kv_wait, origin))
    load_value.wait()

    above = z + 1 < n_z
    below = z >= 1
    up_peer = (ctx_of(lax.rem(z + 1, n_z), line, core), head)
    down_peer = (ctx_of(lax.rem(z + n_z - 1, n_z), line, core), head)

    def ho_copy(way, time, z_at, there):
        return pltpu.make_async_remote_copy(
            src_ref=ho.at[time, z_at],
            dst_ref=ho.at[time, z_at],
            send_sem=ho_send_z.at[way, time, z_at],
            recv_sem=ho_recv.at[time, z_at],
            device_id=there,
            device_id_type=MESH,
        )

    def up_copy(time, z_at):
        return ho_copy(0, time, z_at, up_peer)

    def down_copy(time, z_at):
        return ho_copy(1, time, z_at, down_peer)

    scale = math.log2(math.e) / math.sqrt(NOPE + ROPE)
    n_rows = GROUP * sub

    def attend(time, blocks):
        half = time // groups
        group = lax.rem(time, groups)
        n_keys = blocks * tokens
        keys = kv[pl.ds(0, blocks)].reshape(n_keys, KEYW)
        scores = lax.dot_general(query[time], keys, NT, preferred_element_type=jnp.float32)
        row = lax.broadcasted_iota(jnp.int32, (n_rows, 1), 0)
        last = me * tokens + half * sub + lax.rem(row, sub)
        key_index = lax.broadcasted_iota(jnp.int32, (n_rows, n_keys), 1)
        scores = jnp.where(key_index <= last, scores, masked_value)
        peak = jnp.max(scores, axis=1, keepdims=True)
        weights = jnp.exp2((scores - peak) * scale)
        totals = jnp.sum(weights, axis=1, keepdims=True)
        summed = jnp.dot(
            weights.astype(jnp.bfloat16), keys[:, :LATENT], preferred_element_type=jnp.float32
        )
        latent_out = (summed * (1.0 / totals)).astype(jnp.bfloat16)
        for part in range(GROUP):
            columns = pl.ds(pl.multiple_of((group * GROUP + part) * VDIM, VDIM), VDIM)
            ho[time, z, :, pl.ds(part * VDIM, VDIM)] = jnp.dot(
                latent_out[part * sub : (part + 1) * sub],
                value_up[:, columns],
                preferred_element_type=jnp.float32,
            ).astype(jnp.bfloat16)

    def tick(time, carry):
        @pl.when(time < ticks)
        def _():
            pl.when(2 * z < n_z)(functools.partial(attend, time, n_ctx // 2))
            pl.when(2 * z >= n_z)(functools.partial(attend, time, n_ctx))
            pl.when(above)(lambda: up_copy(time, z).start())
            pl.when(below)(lambda: down_copy(time, z).start())

        for step in range(1, n_z - 1):
            past = time - step - LAG
            in_time = jnp.logical_and(past >= 0, past < ticks)

            @pl.when(jnp.logical_and(in_time, jnp.logical_and(z >= step, above)))
            def _():
                up_copy(past, z - step).wait_recv()
                up_copy(past, z - step).start()

            @pl.when(jnp.logical_and(in_time, jnp.logical_and(z + step < n_z, below)))
            def _():
                down_copy(past, z + step).wait_recv()
                down_copy(past, z + step).start()

        return carry

    lax.fori_loop(0, ticks + n_z - 2 + LAG, tick, 0)

    for index in range(CHUNKS):
        proj_line(index).wait_recv()
        proj_across(index).start()
    load_proj.wait()
    proj_core.wait_recv()
    for index in range(CHUNKS):
        proj_across(index).wait_recv()

    def back(half, z_at):
        return pltpu.make_async_remote_copy(
            src_ref=out_send.at[half, z_at],
            dst_ref=land.at[head, slot, half],
            send_sem=back_send.at[half, z_at],
            recv_sem=land_recv.at[head, slot, half],
            device_id=(ctx_of(z_at, line, core), owner_head),
            device_id_type=MESH,
        )

    stays = owner_head == head

    for half in range(SPLIT):
        acc[...] = jnp.zeros_like(acc)

        def add(group, carry):
            time = half * groups + group
            for step in range(1, n_z):

                @pl.when(jnp.logical_and(z >= step, jnp.logical_or(z == n_z - 1, step == n_z - 1)))
                def _():
                    up_copy(time, z - step).wait_recv()

                @pl.when(jnp.logical_and(z + step < n_z, jnp.logical_or(z == 0, step == n_z - 1)))
                def _():
                    down_copy(time, z + step).wait_recv()

            block = ho[time].reshape(n_z * sub, GROUP * VDIM)
            span = pl.ds(pl.multiple_of(group * (GROUP * VDIM), GROUP * VDIM), GROUP * VDIM)
            for line_at in range(LINES):
                for core_at in range(CORES):
                    acc[line_at, core_at] += lax.dot_general(
                        block,
                        proj[line_at, core_at, :, span],
                        NT,
                        preferred_element_type=jnp.float32,
                    )
            return carry

        lax.fori_loop(0, groups, add, 0)
        for z_at in range(n_z):
            out_send[half, z_at] = acc[:, :, pl.ds(z_at * sub, sub), :].astype(jnp.bfloat16)
        for step in range(1, n_z):
            back(half, z_peer(step)).start()

        @pl.when(stays)
        def _():
            pltpu.make_async_copy(
                out_send.at[half, z], land.at[head, slot, half], land_recv.at[head, slot, half]
            ).start()

        @pl.when(jnp.logical_not(stays))
        def _():
            back(half, z).start()

    for half in range(SPLIT):
        for part in range(n_head):
            for spot in range(spots):
                pltpu.make_async_copy(
                    out_send.at[0, 0], land.at[part, spot, half], land_recv.at[part, spot, half]
                ).wait()
        columns = []
        for spot in range(spots):
            for line_at in range(LINES):
                for core_at in range(CORES):
                    total = land[0, spot, half, line_at, core_at].astype(jnp.float32)
                    for part in range(1, n_head):
                        total += land[part, spot, half, line_at, core_at].astype(jnp.float32)
                    columns.append(total)
        out_ref[pl.ds(half * sub, sub), :] = jnp.concatenate(columns, axis=1).astype(out_ref.dtype)

    for allowed, copy in sends:
        if allowed is None:
            copy.wait_send()
        else:
            pl.when(allowed)(copy.wait_send)
    proj_core.wait_send()
    for index in range(CHUNKS):
        proj_line(index).wait_send()
        proj_across(index).wait_send()

    def drain(time, carry):
        for z_at in range(n_z):
            pl.when(jnp.logical_and(above, z >= z_at))(up_copy(time, z_at).wait_send)
            pl.when(jnp.logical_and(below, z <= z_at))(down_copy(time, z_at).wait_send)
        return carry

    lax.fori_loop(0, ticks, drain, 0)
    for half in range(SPLIT):
        for step in range(1, n_z):
            back(half, z_peer(step)).wait_send()
        pl.when(jnp.logical_not(stays))(back(half, z).wait_send)


def body(
    n_ctx,
    n_head,
    queries_nope,
    queries_rope,
    latents,
    rope_keys,
    positions,
    key_up,
    value_up,
    out_proj,
):
    tokens = latents.shape[0]
    heads = key_up.shape[1] // NOPE
    groups = heads // GROUP
    n_z = n_ctx // (CORES * LINES)
    spots = n_z // n_head
    sub = tokens // SPLIT
    width = out_proj.shape[1]
    bf16 = jnp.bfloat16
    cosine, sine = rope_tables(positions, ROPE)
    cosine = jnp.concatenate([cosine] * 4, axis=1)
    sine = jnp.concatenate([-sine, sine] * 2, axis=1)
    out_proj = out_proj.T
    vmem = pl.BlockSpec(memory_space=pltpu.VMEM)
    hbm = pl.BlockSpec(memory_space=pl.ANY)
    dma = pltpu.SemaphoreType.DMA
    rows = n_ctx * tokens * heads * tokens
    return pl.pallas_call(
        functools.partial(kernel, n_ctx, n_head),
        out_shape=jax.ShapeDtypeStruct((tokens, spots * LINES * CORES * width), bf16),
        in_specs=[hbm] * 2 + [vmem] * 2 + [hbm] * 5,
        out_specs=vmem,
        scratch_shapes=[
            pltpu.VMEM(latents.shape, bf16),
            pltpu.VMEM(rope_keys.shape, bf16),
            pltpu.VMEM((tokens, KEYW - LATENT), jnp.float32),
            pltpu.VMEM(queries_nope.shape, bf16),
            pltpu.VMEM(queries_rope.shape, bf16),
            pltpu.VMEM(key_up.shape, bf16),
            pltpu.VMEM(value_up.shape, bf16),
            pltpu.VMEM((LINES, CORES) + out_proj.shape, bf16),
            pltpu.VMEM((n_ctx, tokens, KEYW), bf16),
            pltpu.VMEM((SPLIT * groups, GROUP * sub, KEYW), bf16),
            pltpu.VMEM((SPLIT * groups, n_z, sub, GROUP * VDIM), bf16),
            pltpu.VMEM((LINES, CORES, n_z * sub, width), jnp.float32),
            pltpu.VMEM((SPLIT, n_z, LINES, CORES, sub, width), bf16),
            pltpu.VMEM((n_head, spots, SPLIT, LINES, CORES, sub, width), bf16),
            dma((7,)),
            dma,
            dma((CHUNKS,)),
            dma((CHUNKS,)),
            dma,
            dma((CHUNKS,)),
            dma((CHUNKS,)),
            dma((n_z,)),
            dma((n_z,)),
            dma((LINES, n_z)),
            dma((n_ctx,)),
            dma((2, SPLIT * groups, n_z)),
            dma((SPLIT * groups, n_z)),
            dma((SPLIT, n_z)),
            dma((n_head, spots, SPLIT)),
        ],
        compiler_params=pltpu.CompilerParams(
            collective_id=0, has_side_effects=True, vmem_limit_bytes=52 * 1024 * 1024
        ),
        cost_estimate=pl.CostEstimate(
            flops=2 * rows * (KEYW + LATENT), bytes_accessed=1 << 24, transcendentals=rows
        ),
    )(latents, rope_keys, cosine, sine, queries_nope, queries_rope, key_up, value_up, out_proj)


def solution(mesh):
    in_specs = (
        P("ctx", "head"),
        P("ctx", "head"),
        P("ctx", None),
        P("ctx", None),
        P("ctx"),
        P(None, "head"),
        P(None, "head"),
        P("head", "ctx"),
    )
    out_specs = P("ctx", "head")
    run = functools.partial(body, mesh.shape["ctx"], mesh.shape["head"])
    return jax.shard_map(run, mesh=mesh, in_specs=in_specs, out_specs=out_specs, check_vma=False)
```
